32 devices in a mesh: dp: 16 (over z, y, core), mp: 2 (over x).
Axes of the slice: x: 2, y: 2, z: 4, core: 2. Of those that a mesh axis runs over, the one named last changes fastest.
Arguments:
- tokens: bfloat16 [6144, 2048], P('dp'), may hold values from -6 to 6
- doc_ids: int32 [16, 384], P('dp'), may hold values from 0 to 2, never falling along the last dimension, each value on 1 to 192 neighbouring positions
- frame_ids: int32 [16, 384], P('dp'), may hold values from 0 to 5, never falling along the last dimension, each value on 1 to 192 neighbouring positions
- gain_attn: float32 [2048], P('dp'), may hold values from 0.1 to 1.9
- w_query: bfloat16 [2048, 2048], P('dp', 'mp'), may hold values from -0.125 to 0.125
- w_key: bfloat16 [2048, 2048], P('dp', 'mp'), may hold values from -0.125 to 0.125
- w_value: bfloat16 [2048, 2048], P('dp', 'mp'), may hold values from -0.125 to 0.125
- w_output: bfloat16 [2048, 2048], P('mp', 'dp'), may hold values from -0.75 to 0.75
- gain_mlp: float32 [2048], P('dp'), may hold values from 0.1 to 1.9
- w_up: bfloat16 [2048, 8192], P('dp', 'mp'), may hold values from -0.125 to 0.125
- w_down: bfloat16 [8192, 2048], P('mp', 'dp'), may hold values from -0.09375 to 0.09375
- d_out: bfloat16 [6144, 2048], P('dp'), may hold values from -6 to 6
Outputs:
- result: float32 [6144, 2048], P('dp')
- d_tokens: float32 [6144, 2048], P('dp')
- d_gain_attn: float32 [2048], P('dp')
- d_w_query: float32 [2048, 2048], P('dp', 'mp')
- d_w_key: float32 [2048, 2048], P('dp', 'mp')
- d_w_value: float32 [2048, 2048], P('dp', 'mp')
- d_w_output: float32 [2048, 2048], P('mp', 'dp')
- d_gain_mlp: float32 [2048], P('dp')
- d_w_up: float32 [2048, 8192], P('dp', 'mp')
- d_w_down: float32 [8192, 2048], P('mp', 'dp')
The draws below stay inside these ranges and needn't reach their ends.
Inputs may be any that keep to these rules, and one draw needn't show every extreme that they name: `doc_ids`: in each row, document numbers never decrease; every document holds 1 to 192 tokens. `frame_ids`: in each row, frame numbers never decrease; every frame holds 1 to 192 tokens.
All inputs are finite; a program needn't handle non-finite values.
Results may differ from the reference program's by a relative error of at most 0.035.
Values may be sent and summed in bfloat16 or wider, within the bound.
No kernel may reach another device: no remote copies, remote signals or barrier semaphores. Data moves between devices by JAX's collectives and lax.ppermute only.
A program may use at most 320 MiB of HBM per device.

```python
import math
import jax
import jax.numpy as jnp
import numpy as np
from jax import lax

D = 2048
HEAD_DIM = 128
FF = 8192
TOK_DEV = 384
SEQS = 16
TOKENS = 6144
N_DP = 16


def spiked(values, own_key, source, target, blocks, factor):
    def block_of(dim):
        return (jnp.arange(values.shape[dim]) // (values.shape[dim] // blocks)).reshape((-1,) + (1,) * (values.ndim - 1 - dim))

    one_side = jax.random.permutation(own_key, blocks)[block_of(target)]
    second = (block_of(target) + blocks // 2) % blocks
    return jnp.where((block_of(source) == one_side) | (block_of(source) == second), factor * values, values)


def block_levels(rng, extent, cuts, least, largest):
    factor_of = 1.0
    for axis_at, shards_of in cuts:
        steps = jax.random.uniform(jax.random.fold_in(jax.random.fold_in(rng, 6), axis_at), (shards_of,), jnp.float32, least / len(cuts), largest / len(cuts))
        factor_of = factor_of * jnp.repeat(jnp.exp(steps), extent[axis_at] // shards_of).reshape((-1,) + (1,) * (len(extent) - 1 - axis_at))
    return factor_of


def split_up(count, total, limit, lean):
    weights = [(1 << 20) // math.isqrt(rank ** lean) + 1 for rank in range(2, count + 1)]
    rest, counts = total - limit - (count - 1), [1] * (count - 1)
    while rest > 0:
        free = [i for i in range(count - 1) if counts[i] < limit]
        pool, budget = sum([weights[i] for i in free]), rest
        for i in free:
            addition = min(limit - counts[i], max(1, budget * weights[i] // pool), rest)
            counts[i] = counts[i] + addition
            rest = rest - addition
    return np.array([limit] + counts)


def uneven_parts(stream_key, count, total, limit, lean):
    if count == 2:
        one = jax.random.randint(stream_key, (), max(1, total - limit), min(limit, total - 1) + 1)
        return jnp.stack([one, total - one])
    tallies = jnp.asarray(split_up(count, total, limit, lean), jnp.int32)
    pairs = (count - 1) // 2
    donor, sink = tallies[1:1 + 2 * pairs:2], tallies[2:2 + 2 * pairs:2]
    slack = jnp.minimum(donor - 1, limit - sink)
    shifted = jax.random.randint(jax.random.fold_in(stream_key, 1), (pairs,), 0, 1 << 20) % (slack + 1)
    tallies = tallies.at[1:1 + 2 * pairs:2].set(donor - shifted).at[2:2 + 2 * pairs:2].set(sink + shifted)
    return tallies[jax.random.permutation(jax.random.fold_in(stream_key, 2), count)]


def noise(rng, shape, width, bound, cuts=(), dtype=jnp.bfloat16):
    entries = jax.random.normal(rng, shape, jnp.float32) * width
    if len(cuts) > 0:
        entries = block_levels(rng, shape, cuts, -0.22, 0.18) * entries
    return jnp.clip(entries, min=-bound, max=bound).astype(dtype)


def noise_with(own_key, extent, scale, reach, shards, heavy, held_as=jnp.bfloat16):
    values = scale * jax.random.normal(own_key, extent, jnp.float32)
    if shards:
        values = values * block_levels(own_key, extent, shards, -0.22, 0.18)
    return jnp.clip(spiked(values, jax.random.fold_in(own_key, 3), *heavy), -reach, reach).astype(held_as)


def setup_inputs(seed: int = 0) -> dict:
    keys = jax.random.split(jax.random.key(seed), 13)
    return {
        "tokens": noise(keys[0], (TOKENS, D), 1.0, 6.0, ((0, 16),)),
        "doc_ids": jax.vmap(lambda own: jnp.searchsorted(jnp.cumsum(uneven_parts(own, 3, TOK_DEV, TOK_DEV // 2, 1)), jnp.arange(TOK_DEV), side="right"))(jax.random.split(keys[1], SEQS)).reshape((SEQS, TOK_DEV)).astype(jnp.int32),
        "frame_ids": jax.vmap(lambda own: jnp.searchsorted(jnp.cumsum(uneven_parts(own, TOK_DEV // 64, TOK_DEV, TOK_DEV // 2, 1)), jnp.arange(TOK_DEV), side="right"))(jax.random.split(keys[2], SEQS)).reshape((SEQS, TOK_DEV)).astype(jnp.int32),
        "gain_attn": jnp.clip(1.0 + 0.18 * jax.random.normal(keys[3], (D,), jnp.float32), 0.1, 1.9),
        "w_query": noise(keys[4], (D, D), D ** -0.5, 0.125, ((0, 16), (1, 2))),
        "w_key": noise(keys[5], (D, D), D ** -0.5, 0.125, ((0, 16), (1, 2))),
        "w_value": noise(keys[6], (D, D), D ** -0.5, 0.125, ((0, 16), (1, 2))),
        "w_output": noise(keys[7], (D, D), (D // 32) ** -0.5, 0.75, ((0, 2), (1, 16))),
        "gain_mlp": jnp.clip(1.0 + 0.18 * jax.random.normal(keys[8], (D,), jnp.float32), 0.1, 1.9),
        "w_up": noise(keys[9], (D, FF), D ** -0.5, 0.125, ((0, 16), (1, 2))),
        "w_down": noise(keys[10], (FF, D), (FF // 2) ** -0.5, 0.09375, ((0, 2), (1, 16))),
        "d_out": noise_with(keys[11], (TOKENS, D), 1.0, 6.0, ((0, 16),), (0, 1, 16, 2.0)),
    }


@jax.custom_vjp
def low(v):
    return lax.optimization_barrier(v.astype(jnp.bfloat16)).astype(jnp.float32)

@jax.custom_vjp
def low_back(v):
    return v

def low_keep(v):
    return (low(v), None)

def low_pass(kept, grad):
    return (grad,)

def back_keep(v):
    return (v, None)

def back_low(kept, grad):
    return (low(grad),)
low.defvjp(low_keep, low_pass)
low_back.defvjp(back_keep, back_low)
EPSILON = 1e-05
MASKED = -1e+30
HIGHEST_PRECISION = lax.Precision.HIGHEST

def product_plain(factor_one, factor_two):
    return jnp.dot(factor_one, factor_two, precision=HIGHEST_PRECISION)

def layer_norm(values, scale_vec):
    centered = values - lax.optimization_barrier(jnp.mean(values, axis=-1, keepdims=True))
    standard = centered * lax.rsqrt(lax.optimization_barrier(jnp.mean(centered * centered, axis=-1, keepdims=True)) + EPSILON)
    return standard * scale_vec

def block_forward(block_rows, doc_block, frame_block, weights):
    gain_one, query_w, key_w, value_w, output_w, gain_two, up_w, down_w = weights
    group_count, seq_len = doc_block.shape
    normed_one = low(layer_norm(block_rows, gain_one))
    query_heads = low(low_back(product_plain(normed_one, query_w))).reshape(group_count, seq_len, -1, HEAD_DIM)
    key_heads = low(low_back(product_plain(normed_one, key_w))).reshape(group_count, seq_len, -1, HEAD_DIM)
    value_heads = low(low_back(product_plain(normed_one, value_w))).reshape(group_count, seq_len, -1, HEAD_DIM)
    factor = 1.0 / math.sqrt(HEAD_DIM)
    scores = jnp.einsum('gqhe,gkhe->ghqk', query_heads, key_heads, precision=HIGHEST_PRECISION) * factor
    scores = low_back(scores)
    allowed = (doc_block[:, :, None] == doc_block[:, None, :]) & (frame_block[:, None, :] <= frame_block[:, :, None])
    masked = jnp.where(allowed[:, None], scores, MASKED)
    attn_probs = jax.nn.softmax(masked, axis=-1)
    probs_low = low(attn_probs)
    attended = jnp.einsum('ghqk,gkhe->gqhe', probs_low, value_heads, precision=HIGHEST_PRECISION)
    attended = low(low_back(attended.reshape(group_count * seq_len, -1)))
    hidden = block_rows + low_back(product_plain(attended, output_w))
    normed_two = low(layer_norm(hidden, gain_two))
    pre_act = low_back(product_plain(normed_two, up_w))
    act_low = low(jax.nn.gelu(pre_act, approximate=False))
    return hidden + low_back(product_plain(act_low, down_w))

def reference(tokens, doc_ids, frame_ids, gain_attn, w_query, w_key, w_value, w_output, gain_mlp, w_up, w_down, d_out):
    group_size = math.gcd(N_DP, max(1, 4096 // TOK_DEV))
    group_count = N_DP // group_size
    docs_grouped = doc_ids.astype(jnp.int32).reshape(group_count, group_size, TOK_DEV)
    frames_grouped = frame_ids.astype(jnp.int32).reshape(group_count, group_size, TOK_DEV)
    inputs = tokens.astype(jnp.float32).reshape(group_count, group_size * TOK_DEV, D)
    params = jax.tree.map(lambda weight: weight.astype(jnp.float32), (gain_attn, w_query, w_key, w_value, w_output, gain_mlp, w_up, w_down))

    def forward(stacked, weights):

        def one_group(scan_carry, pieces):
            block_rows, doc_block, frame_block = pieces
            return (scan_carry, jax.checkpoint(block_forward)(block_rows, doc_block, frame_block, weights))
        final_carry, outputs = lax.scan(one_group, jnp.zeros((), jnp.float32), (stacked, docs_grouped, frames_grouped))
        return outputs
    outputs, pullback = jax.vjp(forward, inputs, params)
    cotangent = d_out.astype(jnp.float32).reshape(group_count, group_size * TOK_DEV, D)
    grad_inputs, grad_params = pullback(cotangent)
    return (outputs.reshape(TOKENS, D), grad_inputs.reshape(TOKENS, D), grad_params[0], grad_params[1], grad_params[2], grad_params[3], grad_params[4], grad_params[5], grad_params[6], grad_params[7])
```

```python
import functools
import math

import jax
import jax.numpy as jnp
from jax import lax
from jax.sharding import PartitionSpec as P

HEAD_DIM = 128
EPSILON = 1e-05
MASKED = -1e30
LOW = jnp.bfloat16
WIDE = jnp.float32


def plain(one, two):
    return jnp.dot(one, two, preferred_element_type=WIDE)


def inner(one, two):
    return lax.dot_general(one, two, (((0,), (0,)), ((), ())), preferred_element_type=WIDE)


def outer(one, two):
    return lax.dot_general(one, two, (((1,), (1,)), ((), ())), preferred_element_type=WIDE)


def norm_forward(values):
    centered = values - jnp.mean(values, axis=1, keepdims=True)
    inverse = lax.rsqrt(jnp.mean(centered * centered, axis=1, keepdims=True) + EPSILON)
    return centered * inverse, inverse


def norm_backward(scaled, standard, inverse):
    return (
        scaled
        - jnp.mean(scaled, axis=1, keepdims=True)
        - standard * jnp.mean(scaled * standard, axis=1, keepdims=True)
    ) * inverse


def gelu_parts(values):
    half = 0.5 * (1.0 + lax.erf(values * (1.0 / math.sqrt(2.0))))
    slope = half + values * jnp.exp(-0.5 * values * values) * (1.0 / math.sqrt(2.0 * math.pi))
    return values * half, slope


def take(values, index, size, axis):
    return lax.dynamic_slice_in_dim(values, index * size, size, axis)


def put(whole, part, index, axis):
    return lax.dynamic_update_slice_in_dim(whole, part, index * part.shape[axis], axis)


class Links:
    def __init__(self, count):
        self.ring_size = count // 4
        self.to = {k: [(i, i ^ k) for i in range(count)] for k in (1, 2, 3)}
        self.next = [(i, (i + 4) % count) for i in range(count)]
        place = lax.axis_index("dp")
        self.ring_at = place // 4
        self.cell = place % 4
        self.row = self.cell // 2
        self.core = self.cell % 2

    def swap(self, values, k):
        return lax.ppermute(values, "dp", self.to[k])

    def step(self, values):
        return lax.ppermute(values, "dp", self.next)

    def across(self, values):
        return lax.ppermute(values, "mp", [(0, 1), (1, 0)])

    def behind(self, k):
        return lax.rem(self.ring_at - k + 2 * self.ring_size, self.ring_size)


def both_cores(links, own, other, axis):
    return jnp.where(
        links.core == 0,
        jnp.concatenate([own, other], axis=axis),
        jnp.concatenate([other, own], axis=axis),
    )


def gather_pair(links, block, axis):
    size = list(block.shape)
    size[axis] *= 2 * links.ring_size
    whole = jnp.zeros(size, block.dtype)
    for k in range(links.ring_size):
        if k:
            block = links.step(block)
        at = links.behind(k) * 2
        whole = put(whole, block, at + links.row, axis)
        whole = put(whole, links.swap(block, 2), at + 1 - links.row, axis)
    return whole


def gather_ring(links, block, axis):
    size = list(block.shape)
    size[axis] *= links.ring_size
    whole = jnp.zeros(size, block.dtype)
    for k in range(links.ring_size):
        if k:
            block = links.step(block)
        whole = put(whole, block, links.behind(k), axis)
    return whole


def exchange(links, whole, cut_axis, join_axis, finish=lambda part: part, own=None):
    size = whole.shape[cut_axis] // 4
    shape = list(whole.shape)
    shape[cut_axis] = size
    shape[join_axis] *= 4
    parts = [take(whole if own is None else own, links.cell, size, cut_axis)]
    for k in (1, 2, 3):
        parts.append(links.swap(take(whole, links.cell ^ k, size, cut_axis), k))
    parts = [finish(part) for part in parts]
    joined = jnp.zeros(shape, parts[0].dtype)
    for k in range(4):
        joined = put(joined, parts[k], links.cell ^ k, join_axis)
    return joined


def tokens_of_plane(links, own):
    far = links.swap(own, 2)
    return jnp.concatenate([own, links.swap(own, 1), far, links.swap(far, 1)], axis=0)


def sum_over_cores(links, partial):
    rows = partial.shape[0] // 2
    other = links.swap(partial[rows:].astype(LOW), 1)
    return partial[:rows] + other.astype(WIDE)


def sum_across(links, partial):
    low = partial.astype(LOW)
    return low.astype(WIDE) + links.across(low).astype(WIDE)


def sum_over_plane(links, partial):
    rows = partial.shape[0] // 4
    to_core = jnp.concatenate([partial[rows : 2 * rows], partial[3 * rows :]], axis=0).astype(LOW)
    from_core = links.swap(to_core, 1).astype(WIDE)
    far = partial[2 * rows : 3 * rows] + from_core[rows:]
    near = partial[:rows] + from_core[:rows] + links.swap(far.astype(LOW), 2).astype(WIDE)
    return sum_across(links, near)


def shards(
    count,
    tokens,
    doc_ids,
    frame_ids,
    gain_attn,
    w_query,
    w_key,
    w_value,
    w_output,
    gain_mlp,
    w_up,
    w_down,
    d_out,
):
    links = Links(count)
    rows, width = tokens.shape
    ring = links.ring_size
    shard_rows = width // count
    half = w_query.shape[1] // 2
    heads = half // HEAD_DIM

    def scaled_by(weight, gain):
        return (weight.astype(WIDE) * gain[:, None]).astype(LOW)

    halves = [
        scaled_by(weight, gain_attn).reshape(shard_rows, 2, half)
        for weight in (w_query, w_key, w_value)
    ]
    qkv_shard = jnp.concatenate(halves, axis=2)
    qkv_own = lax.dynamic_index_in_dim(qkv_shard, links.core, 1, keepdims=False)
    qkv_other = lax.dynamic_index_in_dim(qkv_shard, 1 - links.core, 1, keepdims=False)
    qkv_block = both_cores(links, qkv_own, links.swap(qkv_other, 1), 0)
    qkv_full = gather_pair(links, qkv_block, 0)

    out_own = take(w_output, links.core, half, 0)
    out_other = take(w_output, 1 - links.core, half, 0)
    out_block = both_cores(links, out_own, links.swap(out_other, 1), 1)
    out_full = gather_pair(links, out_block, 1)

    up_block = exchange(links, scaled_by(w_up, gain_mlp), 1, 0)
    up_full = gather_ring(links, up_block, 0)
    down_block = exchange(links, w_down, 0, 1)
    down_full = gather_ring(links, down_block, 1)

    inputs = tokens.astype(WIDE)
    standard_one, inverse_one = norm_forward(inputs)
    normed_own = standard_one.astype(LOW)
    normed_one = jnp.concatenate([normed_own, links.swap(normed_own, 1)], axis=0)
    docs = jnp.concatenate([doc_ids, links.swap(doc_ids, 1)], axis=0)
    frames = jnp.concatenate([frame_ids, links.swap(frame_ids, 1)], axis=0)
    allowed = (docs[:, :, None] == docs[:, None, :]) & (frames[:, None, :] <= frames[:, :, None])
    qkv = plain(normed_one, qkv_full).astype(LOW)

    def heads_of(values):
        return values.reshape(2, rows, heads, HEAD_DIM)

    query, key, value = (heads_of(qkv[:, i * half : (i + 1) * half]) for i in range(3))
    factor = 1.0 / math.sqrt(HEAD_DIM)
    scores = jnp.einsum("gqhe,gkhe->ghqk", query, key, preferred_element_type=WIDE) * factor
    scores = jnp.where(allowed[:, None], scores, MASKED)
    shifted = jnp.exp(scores - jnp.max(scores, axis=3, keepdims=True))
    probs = shifted / jnp.sum(shifted, axis=3, keepdims=True)
    probs_low = probs.astype(LOW)
    attended = jnp.einsum("ghqk,gkhe->gqhe", probs_low, value, preferred_element_type=WIDE)
    attended = attended.astype(LOW).reshape(2 * rows, half)
    hidden = inputs + sum_across(links, sum_over_cores(links, plain(attended, out_full)))

    standard_two, inverse_two = norm_forward(hidden)
    normed_two = tokens_of_plane(links, standard_two.astype(LOW))
    grad_plane = tokens_of_plane(links, d_out)
    pre_act = plain(normed_two, up_full)
    activated, slope = gelu_parts(pre_act)
    act_low = activated.astype(LOW)
    block = width // ring

    def ring_sum(part_of):
        total = None
        for k in range(1, ring + 1):
            part = part_of(links.behind(k))
            if total is not None:
                part = part + links.step(total.astype(LOW)).astype(WIDE)
            total = part
        return total

    down_sum = ring_sum(lambda at: inner(act_low, take(grad_plane, at, block, 1)))
    result = hidden + sum_over_plane(links, plain(act_low, down_full))
    grad_act = outer(grad_plane, down_full)
    grad_pre = (grad_act * slope).astype(LOW)
    up_sum = ring_sum(lambda at: inner(take(normed_two, at, block, 1), grad_pre))
    scaled_two = sum_over_plane(links, outer(grad_pre, up_full))
    grad_hidden = d_out.astype(WIDE) + norm_backward(scaled_two, standard_two, inverse_two)

    low_own = grad_hidden.astype(LOW)
    grad_low = jnp.concatenate([low_own, links.swap(low_own, 1)], axis=0)
    pair = block // 2

    def pair_sum(part_of, axis):
        total = None
        for k in range(1, ring + 1):
            part = part_of(links.behind(k))
            away = links.swap(take(part, 1 - links.row, pair, axis).astype(LOW), 2)
            part = take(part, links.row, pair, axis) + away.astype(WIDE)
            if total is not None:
                part = part + links.step(total.astype(LOW)).astype(WIDE)
            total = part
        return total

    out_sum = pair_sum(lambda at: inner(attended, take(grad_low, at, block, 1)), 1)
    grad_att = heads_of(outer(grad_low, out_full).astype(LOW))
    grad_probs = jnp.einsum("gqhe,gkhe->ghqk", grad_att, value, preferred_element_type=WIDE)
    delta = jnp.sum(grad_probs * probs, axis=3, keepdims=True)
    grad_scores = (probs * (grad_probs - delta)).astype(LOW)
    grad_query = jnp.einsum("ghqk,gkhe->gqhe", grad_scores, key, preferred_element_type=WIDE)
    grad_key = jnp.einsum("ghqk,gqhe->gkhe", grad_scores, query, preferred_element_type=WIDE)
    grad_value = jnp.einsum("ghqk,gqhe->gkhe", probs_low, grad_att, preferred_element_type=WIDE)
    grad_qkv = jnp.concatenate(
        [
            values.astype(LOW).reshape(2 * rows, half)
            for values in (grad_query * factor, grad_key * factor, grad_value)
        ],
        axis=1,
    )
    qkv_sum = pair_sum(lambda at: inner(take(normed_one, at, block, 1), grad_qkv), 0)
    scaled_one = sum_across(links, sum_over_cores(links, outer(grad_qkv, qkv_full)))
    d_tokens = grad_hidden + norm_backward(scaled_one, standard_one, inverse_one)

    def core_rows(total, axis, join_axis):
        own = take(total, links.core, shard_rows, axis)
        other = links.swap(take(total, 1 - links.core, shard_rows, axis).astype(LOW), 1)
        return both_cores(links, own, other.astype(WIDE), join_axis)

    d_w_output = core_rows(out_sum, 1, 0)
    own = take(qkv_sum, links.core, shard_rows, 0)
    other = links.swap(take(qkv_sum, 1 - links.core, shard_rows, 0).astype(LOW), 1).astype(WIDE)
    raw = [
        both_cores(links, own[:, i * half : (i + 1) * half], other[:, i * half : (i + 1) * half], 1)
        for i in range(3)
    ]
    d_w_query, d_w_key, d_w_value = (part * gain_attn[:, None] for part in raw)
    raw_up = exchange(links, up_sum.astype(LOW), 0, 1, lambda part: part.astype(WIDE), up_sum)
    d_w_up = raw_up * gain_mlp[:, None]
    d_w_down = exchange(links, down_sum.astype(LOW), 1, 0, lambda part: part.astype(WIDE), down_sum)

    def gain_sum(pairs):
        own = sum(jnp.sum(weight.astype(WIDE) * part, axis=1) for weight, part in pairs)
        return own + links.across(own)

    d_gain_attn = gain_sum(zip((w_query, w_key, w_value), raw))
    d_gain_mlp = gain_sum([(w_up, raw_up)])
    return (
        result,
        d_tokens,
        d_gain_attn,
        d_w_query,
        d_w_key,
        d_w_value,
        d_w_output,
        d_gain_mlp,
        d_w_up,
        d_w_down,
    )


def solution(mesh):
    return jax.shard_map(
        functools.partial(shards, mesh.shape["dp"]),
        mesh=mesh,
        in_specs=(
            P("dp", None),
            P("dp", None),
            P("dp", None),
            P("dp"),
            P("dp", "mp"),
            P("dp", "mp"),
            P("dp", "mp"),
            P("mp", "dp"),
            P("dp"),
            P("dp", "mp"),
            P("mp", "dp"),
            P("dp", None),
        ),
        out_specs=(
            P("dp", None),
            P("dp", None),
            P("dp"),
            P("dp", "mp"),
            P("dp", "mp"),
            P("dp", "mp"),
            P("mp", "dp"),
            P("dp"),
            P("dp", "mp"),
            P("mp", "dp"),
        ),
        check_vma=False,
    )
```

```python
import functools
import math

import jax
import jax.numpy as jnp
from jax import lax
from jax.sharding import PartitionSpec as P

HEAD_DIM = 128
EPSILON = 1e-05
MASKED = -1e30
LOW = jnp.bfloat16
WIDE = jnp.float32


def plain(one, two):
    return jnp.dot(one, two, preferred_element_type=WIDE)


def inner(one, two):
    return lax.dot_general(one, two, (((0,), (0,)), ((), ())), preferred_element_type=WIDE)


def outer(one, two):
    return lax.dot_general(one, two, (((1,), (1,)), ((), ())), preferred_element_type=WIDE)


def norm_forward(values):
    centered = values - jnp.mean(values, axis=1, keepdims=True)
    inverse = lax.rsqrt(jnp.mean(centered * centered, axis=1, keepdims=True) + EPSILON)
    return centered * inverse, inverse


def norm_backward(scaled, standard, inverse):
    return (
        scaled
        - jnp.mean(scaled, axis=1, keepdims=True)
        - standard * jnp.mean(scaled * standard, axis=1, keepdims=True)
    ) * inverse


def gelu_parts(values):
    half = 0.5 * (1.0 + lax.erf(values * (1.0 / math.sqrt(2.0))))
    slope = half + values * jnp.exp(-0.5 * values * values) * (1.0 / math.sqrt(2.0 * math.pi))
    return values * half, slope


def take(values, index, size, axis):
    return lax.dynamic_slice_in_dim(values, index * size, size, axis)


def put(whole, part, index, axis):
    return lax.dynamic_update_slice_in_dim(whole, part, index * part.shape[axis], axis)


def wide(values):
    return values.astype(WIDE)


class Order:
    def __init__(self, token):
        self.token = token

    def tie(self, *values):
        tied = lax.optimization_barrier((*values, self.token))[:-1]
        return tied if len(tied) > 1 else tied[0]

    def wait(self, *values):
        *values, self.token = lax.optimization_barrier((*values, self.token))
        return values if len(values) > 1 else values[0]

    def run(self, step, *values):
        values = lax.optimization_barrier((*values, self.token))[:-1]
        results = step(*values)
        if not isinstance(results, tuple):
            return self.wait(results)
        return self.wait(*results)


class Links:
    def __init__(self, count, order):
        self.order = order
        self.ring_size = count // 4
        self.to = {k: [(i, i ^ k) for i in range(count)] for k in (1, 2, 3)}
        self.next = [(i, (i + 4) % count) for i in range(count)]
        place = lax.axis_index("dp")
        self.ring_at = place // 4
        self.cell = place % 4
        self.row = self.cell // 2
        self.core = self.cell % 2

    def swap(self, values, k):
        return lax.ppermute(self.order.tie(values), "dp", self.to[k])

    def step(self, values):
        return lax.ppermute(self.order.tie(values), "dp", self.next)

    def across(self, values):
        return lax.ppermute(self.order.tie(values), "mp", [(0, 1), (1, 0)])

    def behind(self, k):
        return lax.rem(self.ring_at - k + 2 * self.ring_size, self.ring_size)

    def by_core(self, own, other, axis):
        return jnp.where(
            self.core == 0,
            jnp.concatenate([own, other], axis=axis),
            jnp.concatenate([other, own], axis=axis),
        )

    def join(self, parts, axis):
        shape = list(parts[0].shape)
        shape[axis] *= len(parts)
        joined = jnp.zeros(shape, parts[0].dtype)
        for k, part in enumerate(parts):
            joined = put(joined, part, self.cell ^ k, axis)
        return joined

    def lay(self, blocks, axis):
        shape = list(blocks[0].shape)
        shape[axis] *= len(blocks)
        whole = jnp.zeros(shape, blocks[0].dtype)
        for k, block in enumerate(blocks):
            whole = put(whole, block, self.behind(k), axis)
        return whole

    def lay_pairs(self, near, far, axis):
        shape = list(near[0].shape)
        shape[axis] *= 2 * len(near)
        whole = jnp.zeros(shape, near[0].dtype)
        for k in range(len(near)):
            at = self.behind(k) * 2
            whole = put(whole, near[k], at + self.row, axis)
            whole = put(whole, far[k], at + 1 - self.row, axis)
        return whole


def shards(
    count,
    tokens,
    doc_ids,
    frame_ids,
    gain_attn,
    w_query,
    w_key,
    w_value,
    w_output,
    gain_mlp,
    w_up,
    w_down,
    d_out,
):
    order = Order(doc_ids)
    run, wait = order.run, order.wait
    links = Links(count, order)
    swap, step, across = links.swap, links.step, links.across
    ring = links.ring_size
    rows, width = tokens.shape
    owned = width // count
    half = w_query.shape[1] // 2
    heads = half // HEAD_DIM
    hidden_part = w_up.shape[1] // 4
    block = width // ring
    pair = block // 2
    others = range(1, ring)

    chunk = rows // 2

    def chunks(values):
        return values[:chunk], values[chunk:]

    def qkv_shard(core, gain, *weights):
        taken = [(wide(take(w, core, half, 1)) * gain[:, None]).astype(LOW) for w in weights]
        return jnp.concatenate(taken, axis=1)

    qkv_send = run(
        lambda *w: qkv_shard(1 - links.core, *w), gain_attn, w_query, w_key, w_value
    )
    qkv_other = swap(qkv_send, 1)
    out_other = swap(run(lambda w: take(w, 1 - links.core, half, 0), w_output), 1)
    qkv_own = run(lambda *w: qkv_shard(links.core, *w), gain_attn, w_query, w_key, w_value)
    qkv_other, out_other = wait(qkv_other, out_other)
    qkv_block, out_block = run(
        lambda a, b, w, o: (
            links.by_core(a, b, 0),
            links.by_core(take(w, links.core, half, 0), o, 1),
        ),
        qkv_own,
        qkv_other,
        w_output,
        out_other,
    )

    qkv_next, out_next, qkv_far = step(qkv_block), step(out_block), swap(qkv_block, 2)

    def up_shard(weight, gain):
        scaled = (wide(weight) * gain[:, None]).astype(LOW)
        return tuple(take(scaled, links.cell ^ k, hidden_part, 1) for k in (0, 2, 1, 3))

    up_own, up_row, up_core, up_last = run(up_shard, w_up, gain_mlp)
    up_row, up_core = swap(up_row, 2), swap(up_core, 1)
    normed_own = run(lambda x: norm_forward(wide(x))[0].astype(LOW), tokens)
    normed_other = swap(normed_own, 1)
    docs_other, frames_other = swap(doc_ids, 1), swap(frame_ids, 1)

    def put_near(whole, part, k, axis):
        return put(whole, part, links.behind(k) * 2 + links.row, axis)

    def put_far(whole, part, k, axis):
        return put(whole, part, links.behind(k) * 2 + 1 - links.row, axis)

    qkv_full = jnp.zeros((width, 3 * half), LOW)
    out_full = jnp.zeros((half, width), LOW)
    qkv_full, out_full = run(
        lambda q, o, a, b: (put_near(q, a, 0, 0), put_near(o, b, 0, 1)),
        qkv_full,
        out_full,
        qkv_block,
        out_block,
    )
    down_parts = run(
        lambda w: tuple(take(w, links.cell ^ k, hidden_part, 0) for k in range(4)), w_down
    )
    out_blocks = [out_block]
    for k in others:
        if k == 2 or ring < 3:
            qkv_block, out_block, qkv_far, up_row, up_core = wait(
                qkv_next, out_next, qkv_far, up_row, up_core
            )
        elif k == 3:
            qkv_block, out_block, qkv_far, up_last = wait(qkv_next, out_next, qkv_far, up_last)
        else:
            qkv_block, out_block, qkv_far = wait(qkv_next, out_next, qkv_far)
        if k < ring - 1:
            qkv_next, out_next = step(qkv_block), step(out_block)
        qkv_far, far_arrived = swap(qkv_block, 2), qkv_far
        if k == 1:
            up_last = swap(up_last, 3)
        out_blocks.append(out_block)
        if k == ring - 1:
            out_far = swap(out_blocks[0], 2)
            up_block = run(
                lambda *p: links.join(p, 0), up_own, up_core, up_row, up_last
            )
            up_next = step(up_block)
        qkv_full, out_full = run(
            lambda q, o, a, b, f: (
                put_far(put_near(q, a, k, 0), f, k - 1, 0),
                put_near(o, b, k, 1),
            ),
            qkv_full,
            out_full,
            qkv_block,
            out_block,
            far_arrived,
        )
    normed_other, docs_other, frames_other = wait(normed_other, docs_other, frames_other)
    normed_one = run(lambda a, b: jnp.concatenate([a, b], axis=0), normed_own, normed_other)
    up_full = jnp.zeros((width, hidden_part), LOW)
    up_full = run(lambda w, b: put(w, b, links.behind(0), 0), up_full, up_block)
    up_block, qkv_far, out_far = wait(up_next, qkv_far, out_far)
    if ring > 2:
        up_next = step(up_block)
    out_fars = [out_far] + [swap(out_blocks[k], 2) for k in others]
    down_own, down_core, down_row, down_last = down_parts
    down_row = swap(down_row, 2)
    d_out_core = swap(d_out, 1)
    qkv_full = run(lambda w, f: put_far(w, f, ring - 1, 0), qkv_full, qkv_far)
    qkv = run(lambda a, b: plain(a, b).astype(LOW), normed_one, qkv_full)

    def heads_of(values):
        return values.reshape(2, rows, heads, HEAD_DIM)

    factor = 1.0 / math.sqrt(HEAD_DIM)

    def attention(qkv, docs_own, docs_other, frames_own, frames_other):
        docs = jnp.concatenate([docs_own, docs_other], axis=0)
        frames = jnp.concatenate([frames_own, frames_other], axis=0)
        allowed = docs[:, :, None] == docs[:, None, :]
        allowed &= frames[:, None, :] <= frames[:, :, None]
        query, key, value = (heads_of(qkv[:, i * half : (i + 1) * half]) for i in range(3))
        scores = jnp.einsum("gqhe,gkhe->ghqk", query, key, preferred_element_type=WIDE) * factor
        scores = jnp.where(allowed[:, None], scores, MASKED)
        shifted = jnp.exp(scores - jnp.max(scores, axis=3, keepdims=True))
        probs = shifted / jnp.sum(shifted, axis=3, keepdims=True)
        attended = jnp.einsum("ghqk,gkhe->gqhe", probs.astype(LOW), value, preferred_element_type=WIDE)
        return attended.astype(LOW).reshape(2 * rows, half), probs, query, key, value

    attended, probs, query, key, value = run(
        attention, qkv, doc_ids, docs_other, frame_ids, frames_other
    )
    out_full = run(lambda w, f: put_far(w, f, 0, 1), out_full, out_fars[0])
    if ring > 2:
        up_arrived, down_row, *out_fars[1:] = wait(up_next, down_row, *out_fars[1:])
        if ring > 3:
            up_next = step(up_arrived)
    else:
        up_arrived = up_block
        down_row, *out_fars[1:] = wait(down_row, *out_fars[1:])
    down_last, down_core = swap(down_last, 3), swap(down_core, 1)
    d_out_chunks = chunks(d_out)
    d_out_far = [swap(d_out_chunks[0], 2)]

    def put_fars(whole, *fars):
        for k, far in zip(others, fars):
            whole = put_far(whole, far, k, 1)
        return whole

    out_full = run(put_fars, out_full, *out_fars[1:])
    yours = run(lambda a, w: chunks(plain(a[rows:], w).astype(LOW)), attended, out_full)
    yours = [swap(part, 1) for part in yours]
    mine = run(lambda a, w: chunks(plain(a[:rows], w)), attended, out_full)
    out_low, out_cross = [], []
    for j in range(2):
        out_low.append(run(lambda a, b: (a + wide(b)).astype(LOW), mine[j], wait(yours[j])))
        out_cross.append(across(out_low[j]))
    up_full = run(
        lambda w, a, b: put(put(w, a, links.behind(1), 0), b, links.behind(min(2, ring - 1)), 0),
        up_full,
        up_block,
        up_arrived,
    )
    down_last, down_core = wait(down_last, down_core)
    down_block = run(
        lambda *p: links.join(p, 1), down_own, down_core, down_row, down_last
    )
    for k in range(3, ring):
        up_block = wait(up_next)
        if k < ring - 1:
            up_next = step(up_block)
        else:
            down_next = step(down_block)
        if k == ring - 1:
            out_cross[0], d_out_core, d_out_far[0] = wait(out_cross[0], d_out_core, d_out_far[0])
            d_out_far.append(swap(d_out_chunks[1], 2))
        else:
            up_full = run(lambda w, b: put(w, b, links.behind(k), 0), up_full, up_block)
    if ring <= 3:
        out_cross[0], d_out_core, d_out_far[0] = wait(out_cross[0], d_out_core, d_out_far[0])
        d_out_far.append(swap(d_out_chunks[1], 2))
        down_next = step(down_block)
    d_out_last = [swap(d_out_far[0], 1)]

    def second_norm(tokens, low, cross):
        hidden = wide(tokens) + (wide(low) + wide(cross))
        standard, inverse = norm_forward(hidden)
        return hidden, standard, inverse, standard.astype(LOW)

    token_chunks = chunks(tokens)
    seconds, far_two, core_two = [], [], []
    for j in range(2):
        if j:
            out_cross[j] = wait(out_cross[j])
        seconds.append(run(second_norm, token_chunks[j], out_low[j], out_cross[j]))
        far_two.append(swap(seconds[j][3], 2))
        core_two.append(swap(seconds[j][3], 1))
    if ring > 3:
        up_full = run(lambda w, b: put(w, b, links.behind(ring - 1), 0), up_full, up_block)
    down_full = jnp.zeros((hidden_part, width), LOW)
    down_full = run(lambda w, b: put(w, b, links.behind(0), 1), down_full, down_block)
    down_block, d_out_far[1] = wait(down_next, d_out_far[1])
    if ring > 2:
        down_next = step(down_block)
    d_out_last.append(swap(d_out_far[1], 1))
    down_full = run(lambda w, b: put(w, b, links.behind(1), 1), down_full, down_block)
    far_two[0], core_two[0], core_two[1], d_out_last[0] = wait(
        far_two[0], core_two[0], core_two[1], d_out_last[0]
    )
    last_two = [swap(far_two[0], 1)]
    for k in range(2, ring - 1):
        down_block = wait(down_next)
        down_next = step(down_block)
        down_full = run(lambda w, b: put(w, b, links.behind(k), 1), down_full, down_block)
    far_two[1], d_out_last[1] = wait(far_two[1], d_out_last[1])
    last_two.append(swap(far_two[1], 1))
    grad_plane = run(
        lambda *p: jnp.concatenate(p, axis=0), d_out, d_out_core, *d_out_far, *d_out_last
    )
    last_two = wait(*last_two)
    normed_two = run(
        lambda *p: jnp.concatenate(p, axis=0),
        seconds[0][3],
        seconds[1][3],
        *core_two,
        *far_two,
        *last_two,
    )

    def feed_up(normed, weights):
        activated, slope = gelu_parts(plain(normed, weights))
        return activated.astype(LOW), slope.astype(LOW)

    act_low, slope = run(feed_up, normed_two, up_full)

    def part_down(act, grad, k, *arrived):
        part = inner(act, take(grad, links.behind(k), block, 1))
        for total in arrived:
            part = part + wide(total)
        return part.astype(LOW) if k < ring else part

    def part_up(normed, grad, k, *arrived):
        part = inner(take(normed, links.behind(k), block, 1), grad)
        for total in arrived:
            part = part + wide(total)
        return part.astype(LOW) if k < ring else part

    def ring_down(k, *arrived):
        total = run(lambda a, g, *t: part_down(a, g, k, *t), act_low, grad_plane, *arrived)
        return step(total) if k < ring else total

    def ring_up(k, *arrived):
        total = run(lambda n, g, *t: part_up(n, g, k, *t), normed_two, grad_pre, *arrived)
        return step(total) if k < ring else total

    down_sum = ring_down(1)
    if ring > 2:
        down_block = wait(down_next)
        down_full = run(lambda w, b: put(w, b, links.behind(ring - 1), 1), down_full, down_block)
    grad_pre = run(
        lambda g, w, s: (outer(g, w) * wide(s)).astype(LOW), grad_plane, down_full, slope
    )

    def group(product, at, left, weights):
        return chunks(product(left[at * rows : (at + 1) * rows], weights))

    def low_group(product, at, left, weights):
        return tuple(part.astype(LOW) for part in group(product, at, left, weights))

    def pairwise(one, two):
        return [run(lambda a, b: a + wide(b), a, b) for a, b in zip(one, two)]

    def lowered(values):
        return [value.astype(LOW) for value in values]

    last_n = run(lambda a, w: low_group(outer, 3, a, w), grad_pre, up_full)
    last_n = [swap(part, 1) for part in last_n]
    far_own = run(lambda a, w: group(outer, 2, a, w), grad_pre, up_full)
    far_n = []
    for j in range(2):
        far = run(lambda a, b: (a + wide(b)).astype(LOW), far_own[j], wait(last_n[j]))
        far_n.append(swap(far, 2))
    up_sum = ring_up(1)
    core_n = run(lambda a, w: low_group(outer, 1, a, w), grad_pre, up_full)
    core_n = [swap(part, 1) for part in core_n]
    own_n = run(lambda a, w: group(outer, 0, a, w), grad_pre, up_full)
    down_arrived, core_n[0], core_n[1], far_n[0] = wait(down_sum, core_n[0], core_n[1], far_n[0])
    low_n, cross_n = [], []

    def near_sum(own, core, far):
        return (own + wide(core) + wide(far)).astype(LOW)

    low_n.append(run(near_sum, own_n[0], core_n[0], far_n[0]))
    cross_n.append(across(low_n[0]))
    down_sum = ring_down(2, down_arrived)
    last_r = run(lambda a, w: low_group(plain, 3, a, w), act_low, down_full)
    far_n[1] = wait(far_n[1])
    low_n.append(run(near_sum, own_n[1], core_n[1], far_n[1]))
    cross_n.append(across(low_n[1]))
    last_r = [swap(part, 1) for part in last_r]
    core_r = run(lambda a, w: low_group(plain, 1, a, w), act_low, down_full)
    up_arrived, last_r[0], last_r[1] = wait(up_sum, *last_r)
    up_sum = ring_up(2, up_arrived)
    core_r = [swap(part, 1) for part in core_r]
    far_r = run(lambda a, w: group(plain, 2, a, w), act_low, down_full)
    far_r = run(
        lambda a, b, c, d: ((a + wide(c)).astype(LOW), (b + wide(d)).astype(LOW)), *far_r, *last_r
    )
    far_r = [swap(part, 2) for part in far_r]
    own_r = run(lambda a, w: group(plain, 0, a, w), act_low, down_full)

    def second_back(d_out, low, cross, standard, inverse):
        scaled = wide(low) + wide(cross)
        grad_hidden = wide(d_out) + norm_backward(scaled, standard, inverse)
        return grad_hidden, grad_hidden.astype(LOW)

    grad_hidden, low_own, low_other = [], [], []
    if ring > 2:
        down_arrived, cross_n[0], core_r[0], core_r[1] = wait(down_sum, cross_n[0], *core_r)
        down_sum = ring_down(3, down_arrived)
    else:
        cross_n[0], core_r[0], core_r[1] = wait(cross_n[0], *core_r)
    for j in range(2):
        if j:
            cross_n[1] = wait(cross_n[1])
        grad, low = run(
            second_back, d_out_chunks[j], low_n[j], cross_n[j], seconds[j][1], seconds[j][2]
        )
        grad_hidden.append(grad)
        low_own.append(low)
        low_other.append(swap(low, 1))
    if ring > 2:
        up_arrived, far_r[0], far_r[1] = wait(up_sum, *far_r)
        up_sum = ring_up(3, up_arrived)
    else:
        far_r = wait(*far_r)
    low_r, cross_r = [], []
    for j in range(2):
        low_r.append(run(near_sum, own_r[j], core_r[j], far_r[j]))
        cross_r.append(across(low_r[j]))
    low_other = wait(*low_other)
    grad_low = run(lambda *p: jnp.concatenate(p, axis=0), *low_own, *low_other)

    def part_qkv(normed, grad, k):
        part = inner(take(normed, links.behind(k), block, 1), grad)
        return take(part, links.row, pair, 0), take(part, 1 - links.row, pair, 0).astype(LOW)

    def part_out(attended, grad, k):
        part = inner(attended, take(grad, links.behind(k), block, 1))
        return take(part, links.row, pair, 1), take(part, 1 - links.row, pair, 1).astype(LOW)

    out_owns, out_fars = [], []
    for k in range(1, ring + 1):
        own, far = run(lambda a, g: part_out(a, g, k), attended, grad_low)
        out_owns.append(own)
        out_fars.append(swap(far, 2))

    def attention_back(grad_low, out_full, probs, query, key, value):
        grad_att = heads_of(outer(grad_low, out_full).astype(LOW))
        grad_probs = jnp.einsum("gqhe,gkhe->ghqk", grad_att, value, preferred_element_type=WIDE)
        delta = jnp.sum(grad_probs * probs, axis=3, keepdims=True)
        grad_scores = (probs * (grad_probs - delta)).astype(LOW)
        to_query = jnp.einsum("ghqk,gkhe->gqhe", grad_scores, key, preferred_element_type=WIDE)
        to_key = jnp.einsum("ghqk,gqhe->gkhe", grad_scores, query, preferred_element_type=WIDE)
        to_value = jnp.einsum(
            "ghqk,gqhe->gkhe", probs.astype(LOW), grad_att, preferred_element_type=WIDE
        )
        return jnp.concatenate(
            [
                values.astype(LOW).reshape(2 * rows, half)
                for values in (to_query * factor, to_key * factor, to_value)
            ],
            axis=1,
        )

    grad_qkv = run(attention_back, grad_low, out_full, probs, query, key, value)
    qkv_owns, qkv_fars = [], []
    for k in range(1, ring + 1):
        own, far = run(lambda n, g: part_qkv(n, g, k), normed_one, grad_qkv)
        qkv_owns.append(own)
        qkv_fars.append(swap(far, 2) if k < 3 else far)
    out_fars = list(wait(*out_fars))
    out_sum = run(lambda a, b: (a + wide(b)).astype(LOW), out_owns[0], out_fars[0])
    out_next = step(out_sum)

    def first_partial(grad, weights, at):
        return chunks(outer(grad[at * rows : (at + 1) * rows], weights))

    core_m = run(lambda g, w: tuple(lowered(first_partial(g, w, 1))), grad_qkv, qkv_full)
    core_m = [swap(part, 1) for part in core_m]
    own_m = run(lambda g, w: first_partial(g, w, 0), grad_qkv, qkv_full)
    down_arrived = wait(down_sum) if ring > 2 else down_sum
    for k in range(4, ring + 1) if ring > 2 else (2,):
        down_sum = ring_down(k, down_arrived)
        if k < ring:
            down_arrived = wait(down_sum)
    up_arrived = wait(up_sum) if ring > 2 else up_sum
    for k in range(4, ring + 1) if ring > 2 else (2,):
        up_sum = ring_up(k, up_arrived)
        if k < ring:
            up_arrived = wait(up_sum)
    core_m = wait(*core_m)
    low_m, cross_m = [], []
    for j in range(2):
        low_m.append(run(lambda a, b: (a + wide(b)).astype(LOW), own_m[j], core_m[j]))
        cross_m.append(across(low_m[j]))

    def cut(total, axis, size):
        parts = [take(total, links.cell, size, axis)]
        parts += [take(total, links.cell ^ k, size, axis).astype(LOW) for k in (1, 2, 3)]
        return tuple(parts)

    up_ends = list(run(lambda t: cut(t, 0, owned), up_sum))
    down_ends = list(run(lambda t: cut(t, 1, owned), down_sum))

    def add_row(own, far, *arrived):
        total = own + wide(far)
        for part in arrived:
            total = total + wide(part)
        return total

    def add_low(*parts):
        return add_row(*parts).astype(LOW)

    for k in range(1, ring + 1):
        if k == 1:
            qkv_far = wait(qkv_fars[0])
            qkv_sum = run(add_low, qkv_owns[0], qkv_far)
        else:
            qkv_far, qkv_arrived, out_arrived = wait(qkv_fars[k - 1], qkv_next, out_next)
            add = add_low if k < ring else add_row
            qkv_sum, out_sum = run(
                lambda *p: (add(*p[:3]), add(*p[3:])),
                qkv_owns[k - 1],
                qkv_far,
                qkv_arrived,
                out_owns[k - 1],
                out_fars[k - 1],
                out_arrived,
            )
        if k < ring:
            qkv_next = step(qkv_sum)
            if k > 1:
                out_next = step(out_sum)
        if k + 1 < ring:
            qkv_fars[k + 1] = swap(qkv_fars[k + 1], 2)
        if k == 1:
            for j in (1, 2, 3):
                up_ends[j] = swap(up_ends[j], j)
                down_ends[j] = swap(down_ends[j], j)
        if k == 2:
            cross_m = wait(*cross_m)

            def first_back(tokens, grads, lows, crosses):
                standard, inverse = norm_forward(wide(tokens))
                scaled = wide(jnp.concatenate(lows)) + wide(jnp.concatenate(crosses))
                return jnp.concatenate(grads) + norm_backward(scaled, standard, inverse)

            d_tokens = run(
                lambda t, *p: first_back(t, p[:2], p[2:4], p[4:]),
                tokens,
                *grad_hidden,
                *low_m,
                *cross_m,
            )
        if k == min(3, ring):
            up_ends, down_ends = list(wait(*up_ends)), list(wait(*down_ends))

            def up_end(gain, weight, *parts):
                raw = links.join([wide(part) for part in parts], 1)
                return raw * gain[:, None], jnp.sum(wide(weight) * raw, axis=1)

            d_w_up, gain_mlp_own = run(up_end, gain_mlp, w_up, *up_ends)
            gain_mlp_other = across(gain_mlp_own)
            d_w_down = run(lambda *p: links.join([wide(part) for part in p], 0), *down_ends)
            cross_r = wait(*cross_r)
            result = run(
                lambda *p: jnp.concatenate(p[:2])
                + (wide(jnp.concatenate(p[2:4])) + wide(jnp.concatenate(p[4:]))),
                seconds[0][0],
                seconds[1][0],
                *low_r,
                *cross_r,
            )

    def ends(qkv, out):
        return (
            take(qkv, links.core, owned, 0),
            take(qkv, 1 - links.core, owned, 0).astype(LOW),
            take(out, links.core, owned, 1),
            take(out, 1 - links.core, owned, 1).astype(LOW),
        )

    qkv_mine, qkv_yours, out_mine, out_yours = run(ends, qkv_sum, out_sum)
    qkv_yours, out_yours = swap(qkv_yours, 1), swap(out_yours, 1)
    qkv_yours, out_yours = wait(qkv_yours, out_yours)
    d_w_output = links.by_core(out_mine, wide(out_yours), 0)
    raw = [
        links.by_core(qkv_mine[:, at : at + half], wide(qkv_yours[:, at : at + half]), 1)
        for at in (0, half, 2 * half)
    ]
    gain_attn_own = sum(
        jnp.sum(wide(weight) * part, axis=1) for weight, part in zip((w_query, w_key, w_value), raw)
    )
    d_gain_attn = gain_attn_own + across(gain_attn_own)
    d_gain_mlp = gain_mlp_own + gain_mlp_other
    d_w_query, d_w_key, d_w_value = (part * gain_attn[:, None] for part in raw)
    return (
        result,
        d_tokens,
        d_gain_attn,
        d_w_query,
        d_w_key,
        d_w_value,
        d_w_output,
        d_gain_mlp,
        d_w_up,
        d_w_down,
    )


def solution(mesh):
    return jax.shard_map(
        functools.partial(shards, mesh.shape["dp"]),
        mesh=mesh,
        in_specs=(
            P("dp", None),
            P("dp", None),
            P("dp", None),
            P("dp"),
            P("dp", "mp"),
            P("dp", "mp"),
            P("dp", "mp"),
            P("mp", "dp"),
            P("dp"),
            P("dp", "mp"),
            P("mp", "dp"),
            P("dp", None),
        ),
        out_specs=(
            P("dp", None),
            P("dp", None),
            P("dp"),
            P("dp", "mp"),
            P("dp", "mp"),
            P("dp", "mp"),
            P("mp", "dp"),
            P("dp"),
            P("dp", "mp"),
            P("mp", "dp"),
        ),
        check_vma=False,
    )
```

```python
import functools
import math

import jax
import jax.numpy as jnp
from jax import lax
from jax.experimental import pallas as pl
from jax.experimental.pallas import tpu as pltpu
from jax.sharding import PartitionSpec as P

HEAD_DIM = 128
EPSILON = 1e-05
MASKED = -1e30
PIECE = 96
LOW = jnp.bfloat16
WIDE = jnp.float32


def plain(one, two):
    return jnp.dot(one, two, preferred_element_type=WIDE)


def inner(one, two):
    return lax.dot_general(one, two, (((0,), (0,)), ((), ())), preferred_element_type=WIDE)


def outer(one, two):
    return lax.dot_general(one, two, (((1,), (1,)), ((), ())), preferred_element_type=WIDE)


def norm_forward(values):
    centered = values - jnp.mean(values, axis=1, keepdims=True)
    inverse = lax.rsqrt(jnp.mean(centered * centered, axis=1, keepdims=True) + EPSILON)
    return centered * inverse, inverse


def norm_backward(scaled, standard, inverse):
    return (
        scaled
        - jnp.mean(scaled, axis=1, keepdims=True)
        - standard * jnp.mean(scaled * standard, axis=1, keepdims=True)
    ) * inverse


def gelu_parts(values):
    half = 0.5 * (1.0 + lax.erf(values * (1.0 / math.sqrt(2.0))))
    slope = half + values * jnp.exp(-0.5 * values * values) * (1.0 / math.sqrt(2.0 * math.pi))
    return values * half, slope


def take(values, index, size, axis):
    return lax.dynamic_slice_in_dim(values, index * size, size, axis)


def put(whole, part, index, axis):
    return lax.dynamic_update_slice_in_dim(whole, part, index * part.shape[axis], axis)


def wide(values):
    return values.astype(WIDE)


def unscaled_probs(query, key, allowed):
    scores = jnp.where(allowed, outer(query, key) * (1.0 / math.sqrt(HEAD_DIM)), MASKED)
    shifted = jnp.exp(scores - jnp.max(scores, axis=1, keepdims=True))
    return shifted, 1.0 / jnp.sum(shifted, axis=1, keepdims=True)


def head_cuts(heads):
    return [slice(i * HEAD_DIM, (i + 1) * HEAD_DIM) for i in range(heads)]


def attention_forward(query, key, value, doc_row, doc_col, frame_row, frame_col, out):
    allowed = (doc_col[0] == doc_row[0]) & (frame_row[0] <= frame_col[0])
    for cut in head_cuts(out.shape[1] // HEAD_DIM):
        shifted, inverse = unscaled_probs(query[:, cut], key[:, cut], allowed)
        out[:, cut] = plain((shifted * inverse).astype(LOW), value[:, cut]).astype(LOW)


def attention_backward(
    query, key, value, grad, doc_row, doc_col, frame_row, frame_col, to_query, to_key, to_value
):
    allowed = (doc_col[0] == doc_row[0]) & (frame_row[0] <= frame_col[0])
    factor = 1.0 / math.sqrt(HEAD_DIM)
    for cut in head_cuts(grad.shape[1] // HEAD_DIM):
        shifted, inverse = unscaled_probs(query[:, cut], key[:, cut], allowed)
        probs = shifted * inverse
        grad_probs = outer(grad[:, cut], value[:, cut])
        delta = jnp.sum(grad_probs * probs, axis=1, keepdims=True)
        grad_scores = (probs * (grad_probs - delta)).astype(LOW)
        to_query[:, cut] = (plain(grad_scores, key[:, cut]) * factor).astype(LOW)
        to_key[:, cut] = (inner(grad_scores, query[:, cut]) * factor).astype(LOW)
        to_value[:, cut] = inner(probs.astype(LOW), grad[:, cut]).astype(LOW)


def attention_call(kernel, qkv, docs, frames, *grads):
    rows, half = qkv.shape[0] // 2, qkv.shape[1] // 3
    parts = [pl.BlockSpec((rows, half), lambda g, at=at: (g, at)) for at in range(3)]
    along = pl.BlockSpec((1, 1, rows), lambda g: (g, 0, 0))
    down = pl.BlockSpec((1, rows, 1), lambda g: (g, 0, 0))
    shape = jax.ShapeDtypeStruct((2 * rows, half), LOW)
    outs = 3 if grads else 1
    return pl.pallas_call(
        kernel,
        out_shape=[shape] * outs,
        grid=(2,),
        in_specs=parts + parts[:1] * len(grads) + [along, down, along, down],
        out_specs=parts[:1] * outs,
        compiler_params=pltpu.CompilerParams(vmem_limit_bytes=32 << 20),
        cost_estimate=pl.CostEstimate(flops=0, bytes_accessed=0, transcendentals=0),
    )(
        qkv,
        qkv,
        qkv,
        *grads,
        docs[:, None, :],
        docs[:, :, None],
        frames[:, None, :],
        frames[:, :, None],
    )


class Order:
    def __init__(self, token):
        self.token = token

    def tie(self, *values):
        tied = lax.optimization_barrier((*values, self.token))[:-1]
        return tied if len(tied) > 1 else tied[0]

    def wait(self, *values):
        *values, self.token = lax.optimization_barrier((*values, self.token))
        return values if len(values) > 1 else values[0]

    def run(self, step, *values):
        values = lax.optimization_barrier((*values, self.token))[:-1]
        results = step(*values)
        if not isinstance(results, tuple):
            return self.wait(results)
        return self.wait(*results)


class Links:
    def __init__(self, count, order):
        self.order = order
        self.ring_size = count // 4
        self.to = {k: [(i, i ^ k) for i in range(count)] for k in (1, 2, 3)}
        self.next = [(i, (i + 4) % count) for i in range(count)]
        place = lax.axis_index("dp")
        self.ring_at = place // 4
        self.cell = place % 4
        self.row = self.cell // 2
        self.core = self.cell % 2

    def swap(self, values, k):
        return lax.ppermute(self.order.tie(values), "dp", self.to[k])

    def to_core(self, values):
        size = values.shape[0] // max(1, values.shape[0] // PIECE)
        return [self.swap(values[at : at + size], 1) for at in range(0, values.shape[0], size)]

    def step(self, values):
        return lax.ppermute(self.order.tie(values), "dp", self.next)

    def across(self, values):
        return lax.ppermute(self.order.tie(values), "mp", [(0, 1), (1, 0)])

    def behind(self, k):
        return lax.rem(self.ring_at - k + 2 * self.ring_size, self.ring_size)

    def by_core(self, own, other, axis):
        return jnp.where(
            self.core == 0,
            jnp.concatenate([own, other], axis=axis),
            jnp.concatenate([other, own], axis=axis),
        )

    def join(self, parts, axis):
        shape = list(parts[0].shape)
        shape[axis] *= len(parts)
        joined = jnp.zeros(shape, parts[0].dtype)
        for k, part in enumerate(parts):
            joined = put(joined, part, self.cell ^ k, axis)
        return joined

    def lay(self, blocks, axis):
        shape = list(blocks[0].shape)
        shape[axis] *= len(blocks)
        whole = jnp.zeros(shape, blocks[0].dtype)
        for k, block in enumerate(blocks):
            whole = put(whole, block, self.behind(k), axis)
        return whole

    def lay_pairs(self, near, far, axis):
        shape = list(near[0].shape)
        shape[axis] *= 2 * len(near)
        whole = jnp.zeros(shape, near[0].dtype)
        for k in range(len(near)):
            at = self.behind(k) * 2
            whole = put(whole, near[k], at + self.row, axis)
            whole = put(whole, far[k], at + 1 - self.row, axis)
        return whole


def shards(
    count,
    tokens,
    doc_ids,
    frame_ids,
    gain_attn,
    w_query,
    w_key,
    w_value,
    w_output,
    gain_mlp,
    w_up,
    w_down,
    d_out,
):
    order = Order(doc_ids)
    run, wait = order.run, order.wait
    links = Links(count, order)
    swap, step, across = links.swap, links.step, links.across
    ring = links.ring_size
    rows, width = tokens.shape
    owned = width // count
    half = w_query.shape[1] // 2
    heads = half // HEAD_DIM
    hidden_part = w_up.shape[1] // 4
    block = width // ring
    pair = block // 2
    others = range(1, ring)

    chunk = rows // 2

    def chunks(values):
        return values[:chunk], values[chunk:]

    def qkv_shard(core, gain, *weights):
        taken = [(wide(take(w, core, half, 1)) * gain[:, None]).astype(LOW) for w in weights]
        return jnp.concatenate(taken, axis=1)

    qkv_send = run(
        lambda *w: qkv_shard(1 - links.core, *w), gain_attn, w_query, w_key, w_value
    )
    qkv_other = swap(qkv_send, 1)
    out_other = swap(run(lambda w: take(w, 1 - links.core, half, 0), w_output), 1)
    qkv_own = run(lambda *w: qkv_shard(links.core, *w), gain_attn, w_query, w_key, w_value)
    qkv_other, out_other = wait(qkv_other, out_other)
    qkv_block, out_block = run(
        lambda a, b, w, o: (
            links.by_core(a, b, 0),
            links.by_core(take(w, links.core, half, 0), o, 1),
        ),
        qkv_own,
        qkv_other,
        w_output,
        out_other,
    )

    def up_shard(weight, gain):
        scaled = (wide(weight) * gain[:, None]).astype(LOW)
        return tuple(take(scaled, links.cell ^ k, hidden_part, 1) for k in (0, 2, 1, 3))

    def put_near(whole, part, k, axis):
        return put(whole, part, links.behind(k) * 2 + links.row, axis)

    def put_far(whole, part, k, axis):
        return put(whole, part, links.behind(k) * 2 + 1 - links.row, axis)

    qkv_next, out_next, qkv_far = step(qkv_block), step(out_block), swap(qkv_block, 2)
    up_own, up_row, up_core, up_last = run(up_shard, w_up, gain_mlp)
    up_row, up_core = swap(up_row, 2), swap(up_core, 1)
    normed_own = run(lambda x: norm_forward(wide(x))[0].astype(LOW), tokens)
    normed_other = swap(normed_own, 1)
    docs_other, frames_other = swap(doc_ids, 1), swap(frame_ids, 1)
    qkv_full = jnp.zeros((width, 3 * half), LOW)
    out_full = jnp.zeros((half, width), LOW)
    qkv_full, out_full = run(
        lambda q, o, a, b: (put_near(q, a, 0, 0), put_near(o, b, 0, 1)),
        qkv_full,
        out_full,
        qkv_block,
        out_block,
    )
    down_own, down_row, down_core, down_last = run(
        lambda w: tuple(take(w, links.cell ^ k, hidden_part, 0) for k in (0, 2, 1, 3)), w_down
    )
    out_blocks = [out_block]
    for k in others:
        arriving = [qkv_next, out_next, qkv_far]
        if k == 1:
            arriving += [up_row, up_core]
        if k == 2:
            arriving += [up_last]
        if k == 3:
            arriving += [out_far]
        qkv_block, out_block, far_arrived, *arrived = wait(*arriving)
        if k < ring - 1:
            qkv_next, out_next = step(qkv_block), step(out_block)
        elif ring > 2:
            up_next = step(up_block)
        qkv_far = swap(qkv_block, 2)
        out_blocks.append(out_block)
        if k == 1:
            up_row, up_core = arrived
            up_last = swap(up_last, 3)
        if k == 2:
            (up_last,) = arrived
            out_far = swap(out_blocks[0], 2)
        if k == 3:
            (out_far,) = arrived
        if k == ring - 1:
            down_row, down_core = swap(down_row, 2), swap(down_core, 1)
        qkv_full, out_full = run(
            lambda q, o, a, b, f: (
                put_far(put_near(q, a, k, 0), f, k - 1, 0),
                put_near(o, b, k, 1),
            ),
            qkv_full,
            out_full,
            qkv_block,
            out_block,
            far_arrived,
        )
        if k == min(2, ring - 1):
            if ring < 3:
                up_last = wait(up_last)
            up_block = run(lambda *p: links.join(p, 0), up_own, up_core, up_row, up_last)
            if ring < 3:
                up_next = step(up_block)
        if k == 3:
            out_full = run(lambda o, f: put_far(o, f, 0, 1), out_full, out_far)
    normed_other, docs_other, frames_other = wait(normed_other, docs_other, frames_other)
    normed_one = run(lambda a, b: jnp.concatenate([a, b], axis=0), normed_own, normed_other)
    up_full = jnp.zeros((width, hidden_part), LOW)
    up_full = run(lambda w, b: put(w, b, links.behind(0), 0), up_full, up_block)
    up_block, qkv_far, down_row, down_core = wait(up_next, qkv_far, down_row, down_core)
    if ring > 2:
        up_next = step(up_block)
    fars_from = 1 if ring > 3 else 0
    out_fars = [swap(out_blocks[k], 2) for k in range(fars_from, ring)]
    down_last = swap(down_last, 3)
    d_out_core = swap(d_out, 1)
    qkv_full = run(lambda w, f: put_far(w, f, ring - 1, 0), qkv_full, qkv_far)
    qkv = run(lambda a, b: plain(a, b).astype(LOW), normed_one, qkv_full)

    docs = jnp.concatenate([doc_ids, docs_other], axis=0)
    frames = jnp.concatenate([frame_ids, frames_other], axis=0)
    docs, frames = wait(docs, frames)
    attended = run(lambda *v: attention_call(attention_forward, *v)[0], qkv, docs, frames)
    if ring > 2:
        up_arrived, down_last, *out_fars = wait(up_next, down_last, *out_fars)
        if ring > 3:
            up_next = step(up_arrived)
    else:
        up_arrived = up_block
        down_last, *out_fars = wait(down_last, *out_fars)
    d_out_chunks = chunks(d_out)
    d_out_far = [swap(d_out_chunks[0], 2)]

    def put_fars(whole, *fars):
        for k, far in enumerate(fars):
            whole = put_far(whole, far, fars_from + k, 1)
        return whole

    out_full = run(put_fars, out_full, *out_fars)

    def part_of(product, group):
        return lambda left, weights: chunks(
            product(left[group * rows : (group + 1) * rows], weights)
        )

    def low_part_of(product, group):
        part = part_of(product, group)
        return lambda left, weights: tuple(value.astype(LOW) for value in part(left, weights))

    def add_pieces(own, *pieces):
        return own + wide(jnp.concatenate(pieces))

    def add_pieces_low(own, *pieces):
        return add_pieces(own, *pieces).astype(LOW)

    yours = [links.to_core(v) for v in run(low_part_of(plain, 1), attended, out_full)]
    mine = run(part_of(plain, 0), attended, out_full)
    out_low, out_cross = [], []
    for j in range(2):
        out_low.append(run(add_pieces_low, mine[j], *wait(*yours[j])))
        out_cross.append(across(out_low[j]))
    down_block = run(lambda *p: links.join(p, 1), down_own, down_core, down_row, down_last)
    up_full = run(
        lambda w, a, b: put(put(w, a, links.behind(1), 0), b, links.behind(min(2, ring - 1)), 0),
        up_full,
        up_block,
        up_arrived,
    )

    def put_tokens(whole, group, part, *chunk_at):
        at = group * rows + (chunk * chunk_at[0] if chunk_at else 0)
        return lax.dynamic_update_slice_in_dim(whole, part, at, 0)

    grad_plane = jnp.zeros((4 * rows, width), LOW)
    grad_plane = run(lambda w, a: put_tokens(w, 0, a), grad_plane, d_out)
    down_full = jnp.zeros((hidden_part, width), LOW)
    down_full = run(lambda w, b: put(w, b, links.behind(0), 1), down_full, down_block)
    for k in range(3, ring):
        up_block = wait(up_next)
        if k < ring - 1:
            up_next = step(up_block)
            up_full = run(lambda w, b: put(w, b, links.behind(k), 0), up_full, up_block)
    down_next = step(down_block)
    if ring > 3:
        up_full = run(lambda w, b: put(w, b, links.behind(ring - 1), 0), up_full, up_block)

    def second_norm(tokens, low, cross):
        hidden = wide(tokens) + (wide(low) + wide(cross))
        standard, inverse = norm_forward(hidden)
        return hidden, standard, inverse, standard.astype(LOW)

    token_chunks = chunks(tokens)
    seconds, far_two, core_two, last_two = [], [], [], []
    normed_two = jnp.zeros((4 * rows, width), LOW)
    for j in range(2):
        out_cross[j] = wait(out_cross[j])
        seconds.append(run(second_norm, token_chunks[j], out_low[j], out_cross[j]))
        far_two.append(swap(seconds[j][3], 2))
        core_two.append(swap(seconds[j][3], 1))
        normed_two = run(lambda w, a: put_tokens(w, 0, a, j), normed_two, seconds[j][3])
    d_out_core, d_out_far[0] = wait(d_out_core, d_out_far[0])
    down_block = wait(down_next)
    if ring > 2:
        down_next = step(down_block)
    d_out_far.append(swap(d_out_chunks[1], 2))
    d_out_last = [swap(d_out_far[0], 1)]
    down_full, grad_plane = run(
        lambda w, b, g, x, y: (
            put(w, b, links.behind(1), 1),
            put_tokens(put_tokens(g, 1, x), 2, y, 0),
        ),
        down_full,
        down_block,
        grad_plane,
        d_out_core,
        d_out_far[0],
    )
    far_two[0], core_two[0] = wait(far_two[0], core_two[0])
    last_two.append(swap(far_two[0], 1))
    normed_two = run(
        lambda w, a, b: put_tokens(put_tokens(w, 1, a, 0), 2, b, 0),
        normed_two,
        core_two[0],
        far_two[0],
    )
    for k in range(2, ring - 1):
        down_block = wait(down_next)
        down_next = step(down_block)
        down_full = run(lambda w, b: put(w, b, links.behind(k), 1), down_full, down_block)
    far_two[1], core_two[1], last_two[0] = wait(far_two[1], core_two[1], last_two[0])
    last_pieces = links.to_core(far_two[1])
    normed_two = run(
        lambda w, a, b, c: put_tokens(
            put_tokens(put_tokens(w, 1, a, 1), 2, b, 1), 3, c, 0
        ),
        normed_two,
        core_two[1],
        far_two[1],
        last_two[0],
    )
    last_pieces = wait(*last_pieces)
    normed_two = run(
        lambda w, *p: put_tokens(w, 3, jnp.concatenate(p), 1), normed_two, *last_pieces
    )
    d_out_far[1], d_out_last[0] = wait(d_out_far[1], d_out_last[0])
    d_out_pieces = links.to_core(d_out_far[1])

    def feed_up(normed, weights):
        activated, slope = gelu_parts(plain(normed, weights))
        return activated.astype(LOW), slope.astype(LOW)

    act_low, slope = run(feed_up, normed_two, up_full)

    def part_down(act, grad, k, *arrived):
        part = inner(act, take(grad, links.behind(k), block, 1))
        for total in arrived:
            part = part + wide(total)
        return part.astype(LOW) if k < ring else part

    def part_up(normed, grad, k, *arrived):
        part = inner(take(normed, links.behind(k), block, 1), grad)
        for total in arrived:
            part = part + wide(total)
        return part.astype(LOW) if k < ring else part

    def ring_down(k, *arrived):
        total = run(lambda a, g, *t: part_down(a, g, k, *t), act_low, grad_plane, *arrived)
        return step(total) if k < ring else total

    def ring_up(k, *arrived):
        total = run(lambda n, g, *t: part_up(n, g, k, *t), normed_two, grad_pre, *arrived)
        return step(total) if k < ring else total

    d_out_pieces = wait(*d_out_pieces)
    grad_plane = run(
        lambda w, a, b, *p: put_tokens(
            put_tokens(put_tokens(w, 2, a, 1), 3, b, 0), 3, jnp.concatenate(p), 1
        ),
        grad_plane,
        d_out_far[1],
        d_out_last[0],
        *d_out_pieces,
    )
    down_sum = ring_down(1)
    if ring > 2:
        down_block = wait(down_next)
        down_full = run(lambda w, b: put(w, b, links.behind(ring - 1), 1), down_full, down_block)
    grad_pre = run(
        lambda g, w, s: (outer(g, w) * wide(s)).astype(LOW), grad_plane, down_full, slope
    )

    def near_sum(near, far):
        return (near + wide(far)).astype(LOW)

    last_n = [links.to_core(v) for v in run(low_part_of(outer, 3), grad_pre, up_full)]
    far_n = run(part_of(outer, 2), grad_pre, up_full)
    far_n = [
        swap(run(add_pieces_low, far_n[j], *wait(*last_n[j])), 2) for j in range(2)
    ]
    up_sum = ring_up(1)
    down_arrived = wait(down_sum)
    down_sum = ring_down(2, down_arrived)
    core_n = [links.to_core(v) for v in run(low_part_of(outer, 1), grad_pre, up_full)]
    own_n = run(part_of(outer, 0), grad_pre, up_full)
    near_n = [run(add_pieces, own_n[j], *wait(*core_n[j])) for j in range(2)]
    last_r = [links.to_core(v) for v in run(low_part_of(plain, 3), act_low, down_full)]
    far_r = run(part_of(plain, 2), act_low, down_full)
    far_r = [run(add_pieces_low, far_r[j], *wait(*last_r[j])) for j in range(2)]
    low_n, cross_n = [], []
    far_n[0] = wait(far_n[0])
    low_n.append(run(near_sum, near_n[0], far_n[0]))
    cross_n.append(across(low_n[0]))
    up_arrived = wait(up_sum)
    up_sum = ring_up(2, up_arrived)
    far_n[1] = wait(far_n[1])
    low_n.append(run(near_sum, near_n[1], far_n[1]))
    cross_n.append(across(low_n[1]))
    far_r = [swap(part, 2) for part in far_r]
    core_r = [links.to_core(v) for v in run(low_part_of(plain, 1), act_low, down_full)]
    own_r = run(part_of(plain, 0), act_low, down_full)
    near_r = [run(add_pieces, own_r[j], *wait(*core_r[j])) for j in range(2)]
    grad_hidden, grad_low = [], jnp.zeros((2 * rows, width), LOW)
    low_r, cross_r = [], []
    for j in range(2):
        cross_n[j] = wait(cross_n[j])

        def second_back(d_out, low, cross, standard, inverse):
            scaled = wide(low) + wide(cross)
            grad_hidden = wide(d_out) + norm_backward(scaled, standard, inverse)
            return grad_hidden, grad_hidden.astype(LOW)

        grad, low = run(
            second_back, d_out_chunks[j], low_n[j], cross_n[j], seconds[j][1], seconds[j][2]
        )
        other = links.to_core(low)
        grad_hidden.append(grad)
        if j == 0 and ring > 2:
            down_arrived = wait(down_sum)
            down_sum = ring_down(3, down_arrived)
        if j == 1:
            far_r = wait(*far_r)
            for i in range(2):
                low_r.append(run(near_sum, near_r[i], far_r[i]))
                cross_r.append(across(low_r[i]))
        grad_low = run(
            lambda w, a, *p: put_tokens(put_tokens(w, 0, a, j), 1, jnp.concatenate(p), j),
            grad_low,
            low,
            *wait(*other),
        )
    if ring > 2:
        up_arrived = wait(up_sum)
        up_sum = ring_up(3, up_arrived)

    def part_qkv(normed, grad, k):
        part = inner(take(normed, links.behind(k), block, 1), grad)
        return take(part, links.row, pair, 0), take(part, 1 - links.row, pair, 0).astype(LOW)

    def part_out(attended, grad, k):
        part = inner(attended, take(grad, links.behind(k), block, 1))
        return take(part, links.row, pair, 1), take(part, 1 - links.row, pair, 1).astype(LOW)

    out_owns, out_fars = [], []
    for k in range(1, ring + 1):
        own, far = run(lambda a, g: part_out(a, g, k), attended, grad_low)
        out_owns.append(own)
        out_fars.append(swap(far, 2))

    grad_att = run(lambda g, w: outer(g, w).astype(LOW), grad_low, out_full)
    grad_qkv = run(
        lambda q, d, f, g: jnp.concatenate(attention_call(attention_backward, q, d, f, g), axis=1),
        qkv,
        docs,
        frames,
        grad_att,
    )

    def add_row(own, far, *arrived):
        total = own + wide(far)
        for part in arrived:
            total = total + wide(part)
        return total

    def add_low(*parts):
        return add_row(*parts).astype(LOW)

    def cut(total, axis, size):
        parts = [take(total, links.cell, size, axis)]
        parts += [take(total, links.cell ^ k, size, axis).astype(LOW) for k in (1, 2, 3)]
        return tuple(parts)

    def send_ends(total, axis):
        own, *parts = run(lambda t: cut(t, axis, owned), total)
        return [own] + [swap(part, k) for k, part in zip((1, 2, 3), parts)]

    def up_end(gain, weight, *parts):
        raw = links.join([wide(part) for part in parts], 1)
        return raw * gain[:, None], jnp.sum(wide(weight) * raw, axis=1)

    def first_back(tokens, grads, lows, crosses):
        standard, inverse = norm_forward(wide(tokens))
        scaled = wide(jnp.concatenate(lows)) + wide(jnp.concatenate(crosses))
        return jnp.concatenate(grads) + norm_backward(scaled, standard, inverse)

    qkv_owns, qkv_fars = [], []
    for k in range(1, ring + 1):
        own, far = run(lambda n, g: part_qkv(n, g, k), normed_one, grad_qkv)
        qkv_owns.append(own)
        qkv_fars.append(swap(far, 2) if k < 3 else far)
        if k == 2:
            out_fars = wait(*out_fars)
            out_next = step(run(add_low, out_owns[0], out_fars[0]))
    core_m = [links.to_core(v) for v in run(low_part_of(outer, 1), grad_qkv, qkv_full)]
    own_m = run(part_of(outer, 0), grad_qkv, qkv_full)
    low_m = [run(add_pieces_low, own_m[j], *wait(*core_m[j])) for j in range(2)]
    cross_m = [across(part) for part in low_m]
    qkv_far = wait(qkv_fars[0])
    qkv_next = step(run(add_low, qkv_owns[0], qkv_far))
    if ring > 2:
        qkv_fars[2] = swap(qkv_fars[2], 2)
    for k in range(2, ring + 1):
        add = add_low if k < ring else add_row
        out_arrived = wait(out_next)
        out_sum = run(add, out_owns[k - 1], out_fars[k - 1], out_arrived)
        if k < ring:
            out_next = step(out_sum)
        if k == 2:
            down_arrived = wait(down_sum)
            for i in range(4, ring + 1) if ring > 2 else (2,):
                down_sum = ring_down(i, down_arrived)
                if i < ring:
                    down_arrived = wait(down_sum)
            down_ends = send_ends(down_sum, 1)
            cross_r = wait(*cross_r)
        if k == min(3, ring):
            up_arrived = wait(up_sum)
            for i in range(4, ring + 1) if ring > 2 else (2,):
                up_sum = ring_up(i, up_arrived)
                if i < ring:
                    up_arrived = wait(up_sum)
            up_ends = send_ends(up_sum, 0)
        qkv_far = wait(qkv_fars[k - 1])
        qkv_arrived = wait(qkv_next)
        qkv_sum = run(add, qkv_owns[k - 1], qkv_far, qkv_arrived)
        if k < ring:
            qkv_next = step(qkv_sum)
        if k + 1 < ring:
            qkv_fars[k + 1] = swap(qkv_fars[k + 1], 2)
        if k == 2:
            result = run(
                lambda *p: jnp.concatenate(p[:2])
                + (wide(jnp.concatenate(p[2:4])) + wide(jnp.concatenate(p[4:]))),
                seconds[0][0],
                seconds[1][0],
                *low_r,
                *cross_r,
            )
            cross_m = wait(*cross_m)
        if k == min(3, ring):
            d_tokens = run(
                lambda t, *p: first_back(t, p[:2], p[2:4], p[4:]),
                tokens,
                *grad_hidden,
                *low_m,
                *cross_m,
            )
            down_ends = wait(*down_ends)
            d_w_down = run(lambda *p: links.join([wide(part) for part in p], 0), *down_ends)
            up_ends = wait(*up_ends)
            d_w_up, gain_mlp_own = run(up_end, gain_mlp, w_up, *up_ends)
            gain_mlp_other = across(gain_mlp_own)

    def ends(qkv, out):
        return (
            take(qkv, links.core, owned, 0),
            take(qkv, 1 - links.core, owned, 0).astype(LOW),
            take(out, links.core, owned, 1),
            take(out, 1 - links.core, owned, 1).astype(LOW),
        )

    qkv_mine, qkv_yours, out_mine, out_yours = run(ends, qkv_sum, out_sum)
    qkv_yours, out_yours = swap(qkv_yours, 1), swap(out_yours, 1)
    qkv_yours, out_yours = wait(qkv_yours, out_yours)
    d_w_output = links.by_core(out_mine, wide(out_yours), 0)
    raw = [
        links.by_core(qkv_mine[:, at : at + half], wide(qkv_yours[:, at : at + half]), 1)
        for at in (0, half, 2 * half)
    ]
    gain_attn_own = sum(
        jnp.sum(wide(weight) * part, axis=1) for weight, part in zip((w_query, w_key, w_value), raw)
    )
    d_gain_attn = gain_attn_own + across(gain_attn_own)
    d_gain_mlp = gain_mlp_own + gain_mlp_other
    d_w_query, d_w_key, d_w_value = (part * gain_attn[:, None] for part in raw)
    return (
        result,
        d_tokens,
        d_gain_attn,
        d_w_query,
        d_w_key,
        d_w_value,
        d_w_output,
        d_gain_mlp,
        d_w_up,
        d_w_down,
    )


def solution(mesh):
    return jax.shard_map(
        functools.partial(shards, mesh.shape["dp"]),
        mesh=mesh,
        in_specs=(
            P("dp", None),
            P("dp", None),
            P("dp", None),
            P("dp"),
            P("dp", "mp"),
            P("dp", "mp"),
            P("dp", "mp"),
            P("mp", "dp"),
            P("dp"),
            P("dp", "mp"),
            P("mp", "dp"),
            P("dp", None),
        ),
        out_specs=(
            P("dp", None),
            P("dp", None),
            P("dp"),
            P("dp", "mp"),
            P("dp", "mp"),
            P("dp", "mp"),
            P("mp", "dp"),
            P("dp"),
            P("dp", "mp"),
            P("mp", "dp"),
        ),
        check_vma=False,
    )
```

```python
import functools
import math

import jax
import jax.numpy as jnp
from jax import lax
from jax.experimental import pallas as pl
from jax.experimental.pallas import tpu as pltpu
from jax.sharding import PartitionSpec as P

HEAD_DIM = 128
EPSILON = 1e-05
MASKED = -1e30
PIECE = 96
LOW = jnp.bfloat16
WIDE = jnp.float32


def plain(one, two):
    return jnp.dot(one, two, preferred_element_type=WIDE)


def inner(one, two):
    return lax.dot_general(one, two, (((0,), (0,)), ((), ())), preferred_element_type=WIDE)


def outer(one, two):
    return lax.dot_general(one, two, (((1,), (1,)), ((), ())), preferred_element_type=WIDE)


def norm_forward(values):
    centered = values - jnp.mean(values, axis=1, keepdims=True)
    inverse = lax.rsqrt(jnp.mean(centered * centered, axis=1, keepdims=True) + EPSILON)
    return centered * inverse, inverse


def norm_backward(scaled, standard, inverse):
    return (
        scaled
        - jnp.mean(scaled, axis=1, keepdims=True)
        - standard * jnp.mean(scaled * standard, axis=1, keepdims=True)
    ) * inverse


def gelu_parts(values):
    half = 0.5 * (1.0 + lax.erf(values * (1.0 / math.sqrt(2.0))))
    slope = half + values * jnp.exp(-0.5 * values * values) * (1.0 / math.sqrt(2.0 * math.pi))
    return values * half, slope


def take(values, index, size, axis):
    return lax.dynamic_slice_in_dim(values, index * size, size, axis)


def put(whole, part, index, axis):
    return lax.dynamic_update_slice_in_dim(whole, part, index * part.shape[axis], axis)


def wide(values):
    return values.astype(WIDE)


def unscaled_probs(query, key, allowed):
    scores = jnp.where(allowed, outer(query, key) * (1.0 / math.sqrt(HEAD_DIM)), MASKED)
    shifted = jnp.exp(scores - jnp.max(scores, axis=1, keepdims=True))
    return shifted, 1.0 / jnp.sum(shifted, axis=1, keepdims=True)


def head_cuts(heads):
    return [slice(i * HEAD_DIM, (i + 1) * HEAD_DIM) for i in range(heads)]


def attention_forward(query, key, value, doc_row, doc_col, frame_row, frame_col, out):
    allowed = (doc_col[0] == doc_row[0]) & (frame_row[0] <= frame_col[0])
    for cut in head_cuts(out.shape[1] // HEAD_DIM):
        shifted, inverse = unscaled_probs(query[:, cut], key[:, cut], allowed)
        out[:, cut] = plain((shifted * inverse).astype(LOW), value[:, cut]).astype(LOW)


def attention_backward(
    query, key, value, grad, doc_row, doc_col, frame_row, frame_col, to_query, to_key, to_value
):
    allowed = (doc_col[0] == doc_row[0]) & (frame_row[0] <= frame_col[0])
    factor = 1.0 / math.sqrt(HEAD_DIM)
    for cut in head_cuts(grad.shape[1] // HEAD_DIM):
        shifted, inverse = unscaled_probs(query[:, cut], key[:, cut], allowed)
        probs = shifted * inverse
        grad_probs = outer(grad[:, cut], value[:, cut])
        delta = jnp.sum(grad_probs * probs, axis=1, keepdims=True)
        grad_scores = (probs * (grad_probs - delta)).astype(LOW)
        to_query[:, cut] = (plain(grad_scores, key[:, cut]) * factor).astype(LOW)
        to_key[:, cut] = (inner(grad_scores, query[:, cut]) * factor).astype(LOW)
        to_value[:, cut] = inner(probs.astype(LOW), grad[:, cut]).astype(LOW)


def attention_call(kernel, qkv, docs, frames, *grads):
    rows, half = qkv.shape[0] // 2, qkv.shape[1] // 3
    parts = [pl.BlockSpec((rows, half), lambda g, at=at: (g, at)) for at in range(3)]
    along = pl.BlockSpec((1, 1, rows), lambda g: (g, 0, 0))
    down = pl.BlockSpec((1, rows, 1), lambda g: (g, 0, 0))
    shape = jax.ShapeDtypeStruct((2 * rows, half), LOW)
    outs = 3 if grads else 1
    return pl.pallas_call(
        kernel,
        out_shape=[shape] * outs,
        grid=(2,),
        in_specs=parts + parts[:1] * len(grads) + [along, down, along, down],
        out_specs=parts[:1] * outs,
        compiler_params=pltpu.CompilerParams(vmem_limit_bytes=32 << 20),
        cost_estimate=pl.CostEstimate(flops=0, bytes_accessed=0, transcendentals=0),
    )(
        qkv,
        qkv,
        qkv,
        *grads,
        docs[:, None, :],
        docs[:, :, None],
        frames[:, None, :],
        frames[:, :, None],
    )


class Order:
    def __init__(self, token):
        self.token = token

    def tie(self, *values):
        tied = lax.optimization_barrier((*values, self.token))[:-1]
        return tied if len(tied) > 1 else tied[0]

    def wait(self, *values):
        *values, self.token = lax.optimization_barrier((*values, self.token))
        return values if len(values) > 1 else values[0]

    def run(self, step, *values):
        values = lax.optimization_barrier((*values, self.token))[:-1]
        results = step(*values)
        if not isinstance(results, tuple):
            return self.wait(results)
        return self.wait(*results)


class Links:
    def __init__(self, count, order):
        self.order = order
        self.ring_size = count // 4
        self.to = {k: [(i, i ^ k) for i in range(count)] for k in (1, 2, 3)}
        self.next = [(i, (i + 4) % count) for i in range(count)]
        place = lax.axis_index("dp")
        self.ring_at = place // 4
        self.cell = place % 4
        self.row = self.cell // 2
        self.core = self.cell % 2

    def swap(self, values, k):
        return lax.ppermute(self.order.tie(values), "dp", self.to[k])

    def to_core(self, values):
        size = values.shape[0] // max(1, values.shape[0] // PIECE)
        return [self.swap(values[at : at + size], 1) for at in range(0, values.shape[0], size)]

    def step(self, values):
        return lax.ppermute(self.order.tie(values), "dp", self.next)

    def across(self, values):
        return lax.ppermute(self.order.tie(values), "mp", [(0, 1), (1, 0)])

    def behind(self, k):
        return lax.rem(self.ring_at - k + 2 * self.ring_size, self.ring_size)

    def by_core(self, own, other, axis):
        return jnp.where(
            self.core == 0,
            jnp.concatenate([own, other], axis=axis),
            jnp.concatenate([other, own], axis=axis),
        )

    def join(self, parts, axis):
        shape = list(parts[0].shape)
        shape[axis] *= len(parts)
        joined = jnp.zeros(shape, parts[0].dtype)
        for k, part in enumerate(parts):
            joined = put(joined, part, self.cell ^ k, axis)
        return joined

    def lay(self, blocks, axis):
        shape = list(blocks[0].shape)
        shape[axis] *= len(blocks)
        whole = jnp.zeros(shape, blocks[0].dtype)
        for k, block in enumerate(blocks):
            whole = put(whole, block, self.behind(k), axis)
        return whole

    def lay_pairs(self, near, far, axis):
        shape = list(near[0].shape)
        shape[axis] *= 2 * len(near)
        whole = jnp.zeros(shape, near[0].dtype)
        for k in range(len(near)):
            at = self.behind(k) * 2
            whole = put(whole, near[k], at + self.row, axis)
            whole = put(whole, far[k], at + 1 - self.row, axis)
        return whole


def shards(
    count,
    tokens,
    doc_ids,
    frame_ids,
    gain_attn,
    w_query,
    w_key,
    w_value,
    w_output,
    gain_mlp,
    w_up,
    w_down,
    d_out,
):
    order = Order(doc_ids)
    run, wait = order.run, order.wait
    links = Links(count, order)
    swap, step, across = links.swap, links.step, links.across
    ring = links.ring_size
    rows, width = tokens.shape
    owned = width // count
    half = w_query.shape[1] // 2
    heads = half // HEAD_DIM
    hidden_part = w_up.shape[1] // 4
    block = width // ring
    pair = block // 2
    others = range(1, ring)

    chunk = rows // 2

    def chunks(values):
        return values[:chunk], values[chunk:]

    def qkv_shard(core, gain, *weights):
        taken = [(wide(take(w, core, half, 1)) * gain[:, None]).astype(LOW) for w in weights]
        return jnp.concatenate(taken, axis=1)

    qkv_send = run(
        lambda *w: qkv_shard(1 - links.core, *w), gain_attn, w_query, w_key, w_value
    )
    qkv_other = swap(qkv_send, 1)
    out_other = swap(run(lambda w: take(w, 1 - links.core, half, 0), w_output), 1)
    qkv_own = run(lambda *w: qkv_shard(links.core, *w), gain_attn, w_query, w_key, w_value)
    qkv_other, out_other = wait(qkv_other, out_other)
    qkv_block, out_block = run(
        lambda a, b, w, o: (
            links.by_core(a, b, 0),
            links.by_core(take(w, links.core, half, 0), o, 1),
        ),
        qkv_own,
        qkv_other,
        w_output,
        out_other,
    )

    def up_shard(weight, gain):
        scaled = (wide(weight) * gain[:, None]).astype(LOW)
        return tuple(take(scaled, links.cell ^ k, hidden_part, 1) for k in (0, 2, 1, 3))

    def put_near(whole, part, k, axis):
        return put(whole, part, links.behind(k) * 2 + links.row, axis)

    def put_far(whole, part, k, axis):
        return put(whole, part, links.behind(k) * 2 + 1 - links.row, axis)

    qkv_next, out_next, qkv_far = step(qkv_block), step(out_block), swap(qkv_block, 2)
    up_own, up_row, up_core, up_last = run(up_shard, w_up, gain_mlp)
    up_row, up_core = swap(up_row, 2), swap(up_core, 1)
    normed_own = run(lambda x: norm_forward(wide(x))[0].astype(LOW), tokens)
    normed_other = swap(normed_own, 1)
    docs_other, frames_other = swap(doc_ids, 1), swap(frame_ids, 1)
    qkv_full = jnp.zeros((width, 3 * half), LOW)
    out_full = jnp.zeros((half, width), LOW)
    qkv_full, out_full = run(
        lambda q, o, a, b: (put_near(q, a, 0, 0), put_near(o, b, 0, 1)),
        qkv_full,
        out_full,
        qkv_block,
        out_block,
    )
    down_own, down_row, down_core, down_last = run(
        lambda w: tuple(take(w, links.cell ^ k, hidden_part, 0) for k in (0, 2, 1, 3)), w_down
    )
    out_blocks = [out_block]
    for k in others:
        arriving = [qkv_next, out_next, qkv_far]
        if k == 1:
            arriving += [up_row, up_core]
        if k == 2:
            arriving += [up_last]
        if k == 3:
            arriving += [out_far]
        qkv_block, out_block, far_arrived, *arrived = wait(*arriving)
        if k < ring - 1:
            qkv_next, out_next = step(qkv_block), step(out_block)
        elif ring > 2:
            up_next = step(up_block)
        qkv_far = swap(qkv_block, 2)
        out_blocks.append(out_block)
        if k == 1:
            up_row, up_core = arrived
            up_last = swap(up_last, 3)
        if k == 2:
            (up_last,) = arrived
            out_far = swap(out_blocks[0], 2)
        if k == 3:
            (out_far,) = arrived
        if k == ring - 1:
            down_row, down_core = swap(down_row, 2), swap(down_core, 1)
        qkv_full, out_full = run(
            lambda q, o, a, b, f: (
                put_far(put_near(q, a, k, 0), f, k - 1, 0),
                put_near(o, b, k, 1),
            ),
            qkv_full,
            out_full,
            qkv_block,
            out_block,
            far_arrived,
        )
        if k == min(2, ring - 1):
            if ring < 3:
                up_last = wait(up_last)
            up_block = run(lambda *p: links.join(p, 0), up_own, up_core, up_row, up_last)
            if ring < 3:
                up_next = step(up_block)
        if k == 3:
            out_full = run(lambda o, f: put_far(o, f, 0, 1), out_full, out_far)
    normed_other, docs_other, frames_other = wait(normed_other, docs_other, frames_other)
    normed_one = run(lambda a, b: jnp.concatenate([a, b], axis=0), normed_own, normed_other)
    up_full = jnp.zeros((width, hidden_part), LOW)
    up_full = run(lambda w, b: put(w, b, links.behind(0), 0), up_full, up_block)
    up_block, qkv_far, down_row, down_core = wait(up_next, qkv_far, down_row, down_core)
    if ring > 2:
        up_next = step(up_block)
    fars_from = 1 if ring > 3 else 0
    out_fars = [swap(out_blocks[k], 2) for k in range(fars_from, ring)]
    down_last = swap(down_last, 3)
    d_out_core = swap(d_out, 1)
    qkv_full = run(lambda w, f: put_far(w, f, ring - 1, 0), qkv_full, qkv_far)
    qkv = run(lambda a, b: plain(a, b).astype(LOW), normed_one, qkv_full)

    docs = jnp.concatenate([doc_ids, docs_other], axis=0)
    frames = jnp.concatenate([frame_ids, frames_other], axis=0)
    docs, frames = wait(docs, frames)
    attended = run(lambda *v: attention_call(attention_forward, *v)[0], qkv, docs, frames)
    if ring > 2:
        up_arrived, down_last, *out_fars = wait(up_next, down_last, *out_fars)
        if ring > 3:
            up_next = step(up_arrived)
    else:
        up_arrived = up_block
        down_last, *out_fars = wait(down_last, *out_fars)
    d_out_chunks = chunks(d_out)
    d_out_far = [swap(d_out_chunks[0], 2)]

    def put_fars(whole, *fars):
        for k, far in enumerate(fars):
            whole = put_far(whole, far, fars_from + k, 1)
        return whole

    out_full = run(put_fars, out_full, *out_fars)

    def part_of(product, group):
        return lambda left, weights: chunks(
            product(left[group * rows : (group + 1) * rows], weights)
        )

    def low_part_of(product, group):
        part = part_of(product, group)
        return lambda left, weights: tuple(value.astype(LOW) for value in part(left, weights))

    def add_pieces(own, *pieces):
        return own + wide(jnp.concatenate(pieces))

    def add_pieces_low(own, *pieces):
        return add_pieces(own, *pieces).astype(LOW)

    yours = [links.to_core(v) for v in run(low_part_of(plain, 1), attended, out_full)]
    mine = run(part_of(plain, 0), attended, out_full)
    out_low, out_cross = [], []
    for j in range(2):
        out_low.append(run(add_pieces_low, mine[j], *wait(*yours[j])))
        out_cross.append(across(out_low[j]))
    down_block = run(lambda *p: links.join(p, 1), down_own, down_core, down_row, down_last)
    up_full = run(
        lambda w, a, b: put(put(w, a, links.behind(1), 0), b, links.behind(min(2, ring - 1)), 0),
        up_full,
        up_block,
        up_arrived,
    )

    def put_tokens(whole, group, part, *chunk_at):
        at = group * rows + (chunk * chunk_at[0] if chunk_at else 0)
        return lax.dynamic_update_slice_in_dim(whole, part, at, 0)

    grad_plane = jnp.zeros((4 * rows, width), LOW)
    grad_plane = run(lambda w, a: put_tokens(w, 0, a), grad_plane, d_out)
    down_full = jnp.zeros((hidden_part, width), LOW)
    down_full = run(lambda w, b: put(w, b, links.behind(0), 1), down_full, down_block)
    for k in range(3, ring):
        up_block = wait(up_next)
        if k < ring - 1:
            up_next = step(up_block)
            up_full = run(lambda w, b: put(w, b, links.behind(k), 0), up_full, up_block)
    down_next = step(down_block)
    if ring > 3:
        up_full = run(lambda w, b: put(w, b, links.behind(ring - 1), 0), up_full, up_block)

    def second_norm(tokens, low, cross):
        hidden = wide(tokens) + (wide(low) + wide(cross))
        standard, inverse = norm_forward(hidden)
        return hidden, standard, inverse, standard.astype(LOW)

    token_chunks = chunks(tokens)
    seconds, far_two, core_two, last_two = [], [], [], []
    normed_two = jnp.zeros((4 * rows, width), LOW)
    for j in range(2):
        out_cross[j] = wait(out_cross[j])
        seconds.append(run(second_norm, token_chunks[j], out_low[j], out_cross[j]))
        far_two.append(swap(seconds[j][3], 2))
        core_two.append(swap(seconds[j][3], 1))
        normed_two = run(lambda w, a: put_tokens(w, 0, a, j), normed_two, seconds[j][3])
    d_out_core, d_out_far[0] = wait(d_out_core, d_out_far[0])
    down_block = wait(down_next)
    if ring > 2:
        down_next = step(down_block)
    d_out_far.append(swap(d_out_chunks[1], 2))
    d_out_last = [swap(d_out_far[0], 1)]
    down_full, grad_plane = run(
        lambda w, b, g, x, y: (
            put(w, b, links.behind(1), 1),
            put_tokens(put_tokens(g, 1, x), 2, y, 0),
        ),
        down_full,
        down_block,
        grad_plane,
        d_out_core,
        d_out_far[0],
    )
    far_two[0], core_two[0] = wait(far_two[0], core_two[0])
    last_two.append(swap(far_two[0], 1))
    normed_two = run(
        lambda w, a, b: put_tokens(put_tokens(w, 1, a, 0), 2, b, 0),
        normed_two,
        core_two[0],
        far_two[0],
    )
    for k in range(2, ring - 1):
        down_block = wait(down_next)
        down_next = step(down_block)
        down_full = run(lambda w, b: put(w, b, links.behind(k), 1), down_full, down_block)
    far_two[1], core_two[1], last_two[0] = wait(far_two[1], core_two[1], last_two[0])
    last_pieces = links.to_core(far_two[1])
    normed_two = run(
        lambda w, a, b, c: put_tokens(
            put_tokens(put_tokens(w, 1, a, 1), 2, b, 1), 3, c, 0
        ),
        normed_two,
        core_two[1],
        far_two[1],
        last_two[0],
    )
    last_pieces = wait(*last_pieces)
    normed_two = run(
        lambda w, *p: put_tokens(w, 3, jnp.concatenate(p), 1), normed_two, *last_pieces
    )
    d_out_far[1], d_out_last[0] = wait(d_out_far[1], d_out_last[0])
    d_out_pieces = links.to_core(d_out_far[1])

    def feed_up(normed, weights):
        activated, slope = gelu_parts(plain(normed, weights))
        return activated.astype(LOW), slope.astype(LOW)

    act_low, slope = run(feed_up, normed_two, up_full)

    def part_down(act, grad, k, *arrived):
        part = inner(act, take(grad, links.behind(k), block, 1))
        for total in arrived:
            part = part + wide(total)
        return part.astype(LOW) if k < ring else part

    def part_up(normed, grad, k, *arrived):
        part = inner(take(normed, links.behind(k), block, 1), grad)
        for total in arrived:
            part = part + wide(total)
        return part.astype(LOW) if k < ring else part

    def ring_down(k, *arrived):
        total = run(lambda a, g, *t: part_down(a, g, k, *t), act_low, grad_plane, *arrived)
        return step(total) if k < ring else total

    def ring_up(k, *arrived):
        total = run(lambda n, g, *t: part_up(n, g, k, *t), normed_two, grad_pre, *arrived)
        return step(total) if k < ring else total

    d_out_pieces = wait(*d_out_pieces)
    grad_plane = run(
        lambda w, a, b, *p: put_tokens(
            put_tokens(put_tokens(w, 2, a, 1), 3, b, 0), 3, jnp.concatenate(p), 1
        ),
        grad_plane,
        d_out_far[1],
        d_out_last[0],
        *d_out_pieces,
    )
    down_sum = ring_down(1)
    if ring > 2:
        down_block = wait(down_next)
        down_full = run(lambda w, b: put(w, b, links.behind(ring - 1), 1), down_full, down_block)
    grad_pre = run(
        lambda g, w, s: (outer(g, w) * wide(s)).astype(LOW), grad_plane, down_full, slope
    )

    def near_sum(near, far):
        return (near + wide(far)).astype(LOW)

    last_n = [links.to_core(v) for v in run(low_part_of(outer, 3), grad_pre, up_full)]
    far_n = run(part_of(outer, 2), grad_pre, up_full)
    far_a = run(add_pieces_low, far_n[0], *wait(*last_n[0]))
    far_b = run(add_pieces_low, far_n[1], *wait(*last_n[1]))
    far_a = swap(far_a, 2)
    up_sum = ring_up(1)
    down_arrived = wait(down_sum)
    down_sum = ring_down(2, down_arrived)
    far_n = [far_a, swap(far_b, 2)]
    core_n = [links.to_core(v) for v in run(low_part_of(outer, 1), grad_pre, up_full)]
    own_n = run(part_of(outer, 0), grad_pre, up_full)
    near_n = [run(add_pieces, own_n[j], *wait(*core_n[j])) for j in range(2)]
    def second_back(d_out, low, cross, standard, inverse):
        scaled = wide(low) + wide(cross)
        grad_hidden = wide(d_out) + norm_backward(scaled, standard, inverse)
        return grad_hidden, grad_hidden.astype(LOW)

    def back_chunk(j):
        grad, low = run(
            second_back, d_out_chunks[j], low_n[j], cross_n[j], seconds[j][1], seconds[j][2]
        )
        return grad, low, links.to_core(low)

    low_n, cross_n = [], []
    for j in range(2):
        low_n.append(run(near_sum, near_n[j], wait(far_n[j])))
        cross_n.append(across(low_n[j]))
    cross_n[0] = wait(cross_n[0])
    backs = [back_chunk(0)]
    up_arrived = wait(up_sum)
    up_sum = ring_up(2, up_arrived)
    last_r = [links.to_core(v) for v in run(low_part_of(plain, 3), act_low, down_full)]
    core_r = [links.to_core(v) for v in run(low_part_of(plain, 1), act_low, down_full)]
    far_r = run(part_of(plain, 2), act_low, down_full)
    own_r = run(part_of(plain, 0), act_low, down_full)
    far_r = [swap(run(add_pieces_low, far_r[j], *wait(*last_r[j])), 2) for j in range(2)]
    near_r = [run(add_pieces, own_r[j], *wait(*core_r[j])) for j in range(2)]
    cross_n[1] = wait(cross_n[1])
    backs.append(back_chunk(1))
    grad_hidden = [backs[0][0], backs[1][0]]
    down_arrived = wait(down_sum)
    down_sum = ring_down(3, down_arrived)
    pieces = wait(*backs[0][2], *backs[1][2])
    grad_low = run(lambda *p: jnp.concatenate(p, axis=0), backs[0][1], backs[1][1], *pieces)

    def part_qkv(normed, grad, k):
        part = inner(take(normed, links.behind(k), block, 1), grad)
        return take(part, links.row, pair, 0), take(part, 1 - links.row, pair, 0).astype(LOW)

    def part_out(attended, grad, k):
        part = inner(attended, take(grad, links.behind(k), block, 1))
        return take(part, links.row, pair, 1), take(part, 1 - links.row, pair, 1).astype(LOW)

    out_owns, out_fars = [], []
    for k in range(1, ring + 1):
        own, far = run(lambda a, g: part_out(a, g, k), attended, grad_low)
        out_owns.append(own)
        out_fars.append(swap(far, 2))

    up_arrived = wait(up_sum)
    up_sum = ring_up(3, up_arrived)
    grad_att = run(lambda g, w: outer(g, w).astype(LOW), grad_low, out_full)
    grad_qkv = run(
        lambda q, d, f, g: jnp.concatenate(attention_call(attention_backward, q, d, f, g), axis=1),
        qkv,
        docs,
        frames,
        grad_att,
    )

    def add_row(own, far, *arrived):
        total = own + wide(far)
        for part in arrived:
            total = total + wide(part)
        return total

    def add_low(*parts):
        return add_row(*parts).astype(LOW)

    def cut(total, axis, size):
        parts = [take(total, links.cell, size, axis)]
        parts += [take(total, links.cell ^ k, size, axis).astype(LOW) for k in (1, 2, 3)]
        return tuple(parts)

    def up_end(gain, weight, *parts):
        raw = links.join([wide(part) for part in parts], 1)
        return raw * gain[:, None], jnp.sum(wide(weight) * raw, axis=1)

    def first_back(tokens, grads, lows, crosses):
        standard, inverse = norm_forward(wide(tokens))
        scaled = wide(jnp.concatenate(lows)) + wide(jnp.concatenate(crosses))
        return jnp.concatenate(grads) + norm_backward(scaled, standard, inverse)

    qkv_owns, qkv_fars = [], []
    for k in range(1, ring + 1):
        own, far = run(lambda n, g: part_qkv(n, g, k), normed_one, grad_qkv)
        qkv_owns.append(own)
        qkv_fars.append(swap(far, 2) if k == 1 else far)
    *out_fars, far_r[0], far_r[1] = wait(*out_fars, *far_r)
    low_r = [run(near_sum, near_r[j], far_r[j]) for j in range(2)]
    cross_r = [across(part) for part in low_r]
    core_m = [links.to_core(v) for v in run(low_part_of(outer, 1), grad_qkv, qkv_full)]
    own_m = run(part_of(outer, 0), grad_qkv, qkv_full)
    low_m = [run(add_pieces_low, own_m[j], *wait(*core_m[j])) for j in range(2)]
    down_arrived = wait(down_sum)
    for k in range(4, ring + 1):
        down_sum = ring_down(k, down_arrived)
        if k < ring:
            down_arrived = wait(down_sum)
    down_ends = list(run(lambda t: cut(t, 1, owned), down_sum))
    down_ends[1], down_ends[2] = swap(down_ends[1], 1), swap(down_ends[2], 2)
    up_arrived = wait(up_sum)
    for k in range(4, ring + 1):
        up_sum = ring_up(k, up_arrived)
        if k < ring:
            up_arrived = wait(up_sum)
    up_ends = list(run(lambda t: cut(t, 0, owned), up_sum))

    qkv_fars[0], down_ends[1], down_ends[2], cross_r[0] = wait(
        qkv_fars[0], down_ends[1], down_ends[2], cross_r[0]
    )
    qkv_sum, out_sum = run(
        lambda a, b, c, d: (add_low(a, b), add_low(c, d)),
        qkv_owns[0],
        qkv_fars[0],
        out_owns[0],
        out_fars[0],
    )
    for k in range(2, ring + 1):
        sent = [step(qkv_sum), step(out_sum), swap(qkv_fars[k - 1], 2)]
        if k == 2:
            down_ends[3] = swap(down_ends[3], 3)
            cross_m = [across(part) for part in low_m]
            *sent, down_ends[3], cross_r[1] = wait(*sent, down_ends[3], cross_r[1])
        elif k == 3:
            up_ends[1], up_ends[2] = swap(up_ends[1], 1), swap(up_ends[2], 2)
            result = run(
                lambda *p: jnp.concatenate(p[:2])
                + (wide(jnp.concatenate(p[2:4])) + wide(jnp.concatenate(p[4:]))),
                seconds[0][0],
                seconds[1][0],
                *low_r,
                *cross_r,
            )
            d_w_down = run(lambda *p: links.join([wide(part) for part in p], 0), *down_ends)
            *sent, up_ends[1], up_ends[2], cross_m[0], cross_m[1] = wait(
                *sent, up_ends[1], up_ends[2], *cross_m
            )
        elif k == 4:
            up_ends[3] = swap(up_ends[3], 3)
            d_tokens = run(
                lambda t, *p: first_back(t, p[:2], p[2:4], p[4:]),
                tokens,
                *grad_hidden,
                *low_m,
                *cross_m,
            )
            *sent, up_ends[3] = wait(*sent, up_ends[3])
        else:
            sent = wait(*sent)
        add = add_low if k < ring else add_row
        qkv_sum, out_sum = run(
            lambda *p: (add(*p[:3]), add(*p[3:])),
            qkv_owns[k - 1],
            sent[2],
            sent[0],
            out_owns[k - 1],
            out_fars[k - 1],
            sent[1],
        )

    def ends(qkv, out):
        return (
            take(qkv, links.core, owned, 0),
            take(qkv, 1 - links.core, owned, 0).astype(LOW),
            take(out, links.core, owned, 1),
            take(out, 1 - links.core, owned, 1).astype(LOW),
        )

    qkv_mine, qkv_yours, out_mine, out_yours = run(ends, qkv_sum, out_sum)
    qkv_yours, out_yours = swap(qkv_yours, 1), swap(out_yours, 1)
    d_w_up, gain_mlp_own = run(up_end, gain_mlp, w_up, *up_ends)
    gain_mlp_other = across(gain_mlp_own)
    qkv_yours, out_yours = wait(qkv_yours, out_yours)
    d_w_output = links.by_core(out_mine, wide(out_yours), 0)
    raw = [
        links.by_core(qkv_mine[:, at : at + half], wide(qkv_yours[:, at : at + half]), 1)
        for at in (0, half, 2 * half)
    ]
    gain_attn_own = sum(
        jnp.sum(wide(weight) * part, axis=1) for weight, part in zip((w_query, w_key, w_value), raw)
    )
    gain_attn_other = across(gain_attn_own)
    d_gain_attn = gain_attn_own + gain_attn_other
    d_gain_mlp = gain_mlp_own + gain_mlp_other
    d_w_query, d_w_key, d_w_value = (part * gain_attn[:, None] for part in raw)
    return (
        result,
        d_tokens,
        d_gain_attn,
        d_w_query,
        d_w_key,
        d_w_value,
        d_w_output,
        d_gain_mlp,
        d_w_up,
        d_w_down,
    )


def solution(mesh):
    return jax.shard_map(
        functools.partial(shards, mesh.shape["dp"]),
        mesh=mesh,
        in_specs=(
            P("dp", None),
            P("dp", None),
            P("dp", None),
            P("dp"),
            P("dp", "mp"),
            P("dp", "mp"),
            P("dp", "mp"),
            P("mp", "dp"),
            P("dp"),
            P("dp", "mp"),
            P("mp", "dp"),
            P("dp", None),
        ),
        out_specs=(
            P("dp", None),
            P("dp", None),
            P("dp"),
            P("dp", "mp"),
            P("dp", "mp"),
            P("dp", "mp"),
            P("mp", "dp"),
            P("dp"),
            P("dp", "mp"),
            P("mp", "dp"),
        ),
        check_vma=False,
    )
```

```python
import functools
import math

import jax
import jax.numpy as jnp
from jax import lax
from jax.experimental import pallas as pl
from jax.experimental.pallas import tpu as pltpu
from jax.sharding import PartitionSpec as P

HEAD_DIM = 128
EPSILON = 1e-05
MASKED = -1e30
PIECE = 96
LOW = jnp.bfloat16
WIDE = jnp.float32


def plain(one, two):
    return jnp.dot(one, two, preferred_element_type=WIDE)


def inner(one, two):
    return lax.dot_general(one, two, (((0,), (0,)), ((), ())), preferred_element_type=WIDE)


def outer(one, two):
    return lax.dot_general(one, two, (((1,), (1,)), ((), ())), preferred_element_type=WIDE)


def norm_forward(values):
    centered = values - jnp.mean(values, axis=1, keepdims=True)
    inverse = lax.rsqrt(jnp.mean(centered * centered, axis=1, keepdims=True) + EPSILON)
    return centered * inverse, inverse


def norm_backward(scaled, standard, inverse):
    return (
        scaled
        - jnp.mean(scaled, axis=1, keepdims=True)
        - standard * jnp.mean(scaled * standard, axis=1, keepdims=True)
    ) * inverse


def gelu_parts(values):
    half = 0.5 * (1.0 + lax.erf(values * (1.0 / math.sqrt(2.0))))
    slope = half + values * jnp.exp(-0.5 * values * values) * (1.0 / math.sqrt(2.0 * math.pi))
    return values * half, slope


def take(values, index, size, axis):
    return lax.dynamic_slice_in_dim(values, index * size, size, axis)


def put(whole, part, index, axis):
    return lax.dynamic_update_slice_in_dim(whole, part, index * part.shape[axis], axis)


def wide(values):
    return values.astype(WIDE)


def unscaled_probs(query, key, allowed):
    scores = jnp.where(allowed, outer(query, key) * (1.0 / math.sqrt(HEAD_DIM)), MASKED)
    shifted = jnp.exp(scores - jnp.max(scores, axis=1, keepdims=True))
    return shifted, 1.0 / jnp.sum(shifted, axis=1, keepdims=True)


def head_cuts(heads):
    return [slice(i * HEAD_DIM, (i + 1) * HEAD_DIM) for i in range(heads)]


def attention_forward(query, key, value, doc_row, doc_col, frame_row, frame_col, out):
    allowed = (doc_col[0] == doc_row[0]) & (frame_row[0] <= frame_col[0])
    for cut in head_cuts(out.shape[1] // HEAD_DIM):
        shifted, inverse = unscaled_probs(query[:, cut], key[:, cut], allowed)
        out[:, cut] = plain((shifted * inverse).astype(LOW), value[:, cut]).astype(LOW)


def attention_backward(
    query, key, value, grad, doc_row, doc_col, frame_row, frame_col, to_query, to_key, to_value
):
    allowed = (doc_col[0] == doc_row[0]) & (frame_row[0] <= frame_col[0])
    factor = 1.0 / math.sqrt(HEAD_DIM)
    for cut in head_cuts(grad.shape[1] // HEAD_DIM):
        shifted, inverse = unscaled_probs(query[:, cut], key[:, cut], allowed)
        probs = shifted * inverse
        grad_probs = outer(grad[:, cut], value[:, cut])
        delta = jnp.sum(grad_probs * probs, axis=1, keepdims=True)
        grad_scores = (probs * (grad_probs - delta)).astype(LOW)
        to_query[:, cut] = (plain(grad_scores, key[:, cut]) * factor).astype(LOW)
        to_key[:, cut] = (inner(grad_scores, query[:, cut]) * factor).astype(LOW)
        to_value[:, cut] = inner(probs.astype(LOW), grad[:, cut]).astype(LOW)


def attention_call(kernel, qkv, docs, frames, *grads):
    rows, half = qkv.shape[0] // 2, qkv.shape[1] // 3
    parts = [pl.BlockSpec((rows, half), lambda g, at=at: (g, at)) for at in range(3)]
    along = pl.BlockSpec((1, 1, rows), lambda g: (g, 0, 0))
    down = pl.BlockSpec((1, rows, 1), lambda g: (g, 0, 0))
    shape = jax.ShapeDtypeStruct((2 * rows, half), LOW)
    outs = 3 if grads else 1
    return pl.pallas_call(
        kernel,
        out_shape=[shape] * outs,
        grid=(2,),
        in_specs=parts + parts[:1] * len(grads) + [along, down, along, down],
        out_specs=parts[:1] * outs,
        compiler_params=pltpu.CompilerParams(vmem_limit_bytes=32 << 20),
        cost_estimate=pl.CostEstimate(flops=0, bytes_accessed=0, transcendentals=0),
    )(
        qkv,
        qkv,
        qkv,
        *grads,
        docs[:, None, :],
        docs[:, :, None],
        frames[:, None, :],
        frames[:, :, None],
    )


class Order:
    def __init__(self, token):
        self.token = token

    def tie(self, *values):
        tied = lax.optimization_barrier((*values, self.token))[:-1]
        return tied if len(tied) > 1 else tied[0]

    def wait(self, *values):
        *values, self.token = lax.optimization_barrier((*values, self.token))
        return values if len(values) > 1 else values[0]

    def run(self, step, *values):
        values = lax.optimization_barrier((*values, self.token))[:-1]
        results = step(*values)
        if not isinstance(results, tuple):
            return self.wait(results)
        return self.wait(*results)


class Links:
    def __init__(self, count, order):
        self.order = order
        self.ring_size = count // 4
        self.to = {k: [(i, i ^ k) for i in range(count)] for k in (1, 2, 3)}
        self.next = [(i, (i + 4) % count) for i in range(count)]
        place = lax.axis_index("dp")
        self.ring_at = place // 4
        self.cell = place % 4
        self.row = self.cell // 2
        self.core = self.cell % 2

    def swap(self, values, k):
        return lax.ppermute(self.order.tie(values), "dp", self.to[k])

    def to_core(self, values):
        size = values.shape[0] // max(1, values.shape[0] // PIECE)
        return [self.swap(values[at : at + size], 1) for at in range(0, values.shape[0], size)]

    def step(self, values):
        return lax.ppermute(self.order.tie(values), "dp", self.next)

    def across(self, values):
        return lax.ppermute(self.order.tie(values), "mp", [(0, 1), (1, 0)])

    def behind(self, k):
        return lax.rem(self.ring_at - k + 2 * self.ring_size, self.ring_size)

    def by_core(self, own, other, axis):
        return jnp.where(
            self.core == 0,
            jnp.concatenate([own, other], axis=axis),
            jnp.concatenate([other, own], axis=axis),
        )

    def join(self, parts, axis):
        shape = list(parts[0].shape)
        shape[axis] *= len(parts)
        joined = jnp.zeros(shape, parts[0].dtype)
        for k, part in enumerate(parts):
            joined = put(joined, part, self.cell ^ k, axis)
        return joined

    def lay(self, blocks, axis):
        shape = list(blocks[0].shape)
        shape[axis] *= len(blocks)
        whole = jnp.zeros(shape, blocks[0].dtype)
        for k, block in enumerate(blocks):
            whole = put(whole, block, self.behind(k), axis)
        return whole

    def lay_pairs(self, near, far, axis):
        shape = list(near[0].shape)
        shape[axis] *= 2 * len(near)
        whole = jnp.zeros(shape, near[0].dtype)
        for k in range(len(near)):
            at = self.behind(k) * 2
            whole = put(whole, near[k], at + self.row, axis)
            whole = put(whole, far[k], at + 1 - self.row, axis)
        return whole


def shards(
    count,
    tokens,
    doc_ids,
    frame_ids,
    gain_attn,
    w_query,
    w_key,
    w_value,
    w_output,
    gain_mlp,
    w_up,
    w_down,
    d_out,
):
    order = Order(doc_ids)
    run, wait = order.run, order.wait
    links = Links(count, order)
    swap, step, across = links.swap, links.step, links.across
    ring = links.ring_size
    rows, width = tokens.shape
    owned = width // count
    half = w_query.shape[1] // 2
    heads = half // HEAD_DIM
    hidden_part = w_up.shape[1] // 4
    block = width // ring
    pair = block // 2
    others = range(1, ring)

    chunk = rows // 2

    def chunks(values):
        return values[:chunk], values[chunk:]

    def qkv_shard(core, gain, *weights):
        taken = [(wide(take(w, core, half, 1)) * gain[:, None]).astype(LOW) for w in weights]
        return jnp.concatenate(taken, axis=1)

    qkv_send = run(
        lambda *w: qkv_shard(1 - links.core, *w), gain_attn, w_query, w_key, w_value
    )
    qkv_other = swap(qkv_send, 1)
    out_other = swap(run(lambda w: take(w, 1 - links.core, half, 0), w_output), 1)
    qkv_own = run(lambda *w: qkv_shard(links.core, *w), gain_attn, w_query, w_key, w_value)
    qkv_other, out_other = wait(qkv_other, out_other)
    qkv_block, out_block = run(
        lambda a, b, w, o: (
            links.by_core(a, b, 0),
            links.by_core(take(w, links.core, half, 0), o, 1),
        ),
        qkv_own,
        qkv_other,
        w_output,
        out_other,
    )

    def up_shard(weight, gain):
        scaled = (wide(weight) * gain[:, None]).astype(LOW)
        return tuple(take(scaled, links.cell ^ k, hidden_part, 1) for k in (0, 2, 1, 3))

    def put_near(whole, part, k, axis):
        return put(whole, part, links.behind(k) * 2 + links.row, axis)

    def put_far(whole, part, k, axis):
        return put(whole, part, links.behind(k) * 2 + 1 - links.row, axis)

    qkv_next, out_next, qkv_far = step(qkv_block), step(out_block), swap(qkv_block, 2)
    up_own, up_row, up_core, up_last = run(up_shard, w_up, gain_mlp)
    up_row, up_core = swap(up_row, 2), swap(up_core, 1)
    normed_own = run(lambda x: norm_forward(wide(x))[0].astype(LOW), tokens)
    normed_other = swap(normed_own, 1)
    docs_other, frames_other = swap(doc_ids, 1), swap(frame_ids, 1)
    qkv_full = jnp.zeros((width, 3 * half), LOW)
    out_full = jnp.zeros((half, width), LOW)
    qkv_full, out_full = run(
        lambda q, o, a, b: (put_near(q, a, 0, 0), put_near(o, b, 0, 1)),
        qkv_full,
        out_full,
        qkv_block,
        out_block,
    )
    down_own, down_row, down_core, down_last = run(
        lambda w: tuple(take(w, links.cell ^ k, hidden_part, 0) for k in (0, 2, 1, 3)), w_down
    )
    out_blocks = [out_block]
    for k in others:
        arriving = [qkv_next, out_next, qkv_far]
        if k == 1:
            arriving += [up_row, up_core]
        if k == 2:
            arriving += [up_last]
        if k == 3:
            arriving += [out_far]
        qkv_block, out_block, far_arrived, *arrived = wait(*arriving)
        if k < ring - 1:
            qkv_next, out_next = step(qkv_block), step(out_block)
        elif ring > 2:
            up_next = step(up_block)
        qkv_far = swap(qkv_block, 2)
        out_blocks.append(out_block)
        if k == 1:
            up_row, up_core = arrived
            up_last = swap(up_last, 3)
        if k == 2:
            (up_last,) = arrived
            out_far = swap(out_blocks[0], 2)
        if k == 3:
            (out_far,) = arrived
        if k == ring - 1:
            down_row, down_core = swap(down_row, 2), swap(down_core, 1)
        qkv_full, out_full = run(
            lambda q, o, a, b, f: (
                put_far(put_near(q, a, k, 0), f, k - 1, 0),
                put_near(o, b, k, 1),
            ),
            qkv_full,
            out_full,
            qkv_block,
            out_block,
            far_arrived,
        )
        if k == min(2, ring - 1):
            if ring < 3:
                up_last = wait(up_last)
            up_block = run(lambda *p: links.join(p, 0), up_own, up_core, up_row, up_last)
            if ring < 3:
                up_next = step(up_block)
        if k == 3:
            out_full = run(lambda o, f: put_far(o, f, 0, 1), out_full, out_far)
    normed_other, docs_other, frames_other = wait(normed_other, docs_other, frames_other)
    normed_one = run(lambda a, b: jnp.concatenate([a, b], axis=0), normed_own, normed_other)
    up_full = jnp.zeros((width, hidden_part), LOW)
    up_full = run(lambda w, b: put(w, b, links.behind(0), 0), up_full, up_block)
    up_block, qkv_far, down_row, down_core = wait(up_next, qkv_far, down_row, down_core)
    if ring > 2:
        up_next = step(up_block)
    fars_from = 1 if ring > 3 else 0
    out_fars = [swap(out_blocks[k], 2) for k in range(fars_from, ring)]
    down_last = swap(down_last, 3)
    d_out_core = swap(d_out, 1)
    qkv_full = run(lambda w, f: put_far(w, f, ring - 1, 0), qkv_full, qkv_far)
    qkv = run(lambda a, b: plain(a, b).astype(LOW), normed_one, qkv_full)

    docs = jnp.concatenate([doc_ids, docs_other], axis=0)
    frames = jnp.concatenate([frame_ids, frames_other], axis=0)
    docs, frames = wait(docs, frames)
    attended = run(lambda *v: attention_call(attention_forward, *v)[0], qkv, docs, frames)
    if ring > 2:
        up_arrived, down_last, *out_fars = wait(up_next, down_last, *out_fars)
        if ring > 3:
            up_next = step(up_arrived)
    else:
        up_arrived = up_block
        down_last, *out_fars = wait(down_last, *out_fars)
    d_out_chunks = chunks(d_out)
    d_out_far = [swap(d_out_chunks[0], 2)]

    def put_fars(whole, *fars):
        for k, far in enumerate(fars):
            whole = put_far(whole, far, fars_from + k, 1)
        return whole

    out_full = run(put_fars, out_full, *out_fars)

    def part_of(product, group):
        return lambda left, weights: chunks(
            product(left[group * rows : (group + 1) * rows], weights)
        )

    def low_part_of(product, group):
        part = part_of(product, group)
        return lambda left, weights: tuple(value.astype(LOW) for value in part(left, weights))

    def add_pieces(own, *pieces):
        return own + wide(jnp.concatenate(pieces))

    def add_pieces_low(own, *pieces):
        return add_pieces(own, *pieces).astype(LOW)

    yours = [links.to_core(v) for v in run(low_part_of(plain, 1), attended, out_full)]
    mine = run(part_of(plain, 0), attended, out_full)
    out_low, out_cross = [], []
    for j in range(2):
        out_low.append(run(add_pieces_low, mine[j], *wait(*yours[j])))
        out_cross.append(across(out_low[j]))
    down_block = run(lambda *p: links.join(p, 1), down_own, down_core, down_row, down_last)
    up_full = run(
        lambda w, a, b: put(put(w, a, links.behind(1), 0), b, links.behind(min(2, ring - 1)), 0),
        up_full,
        up_block,
        up_arrived,
    )

    def put_tokens(whole, group, part, *chunk_at):
        at = group * rows + (chunk * chunk_at[0] if chunk_at else 0)
        return lax.dynamic_update_slice_in_dim(whole, part, at, 0)

    grad_plane = jnp.zeros((4 * rows, width), LOW)
    grad_plane = run(lambda w, a: put_tokens(w, 0, a), grad_plane, d_out)
    down_full = jnp.zeros((hidden_part, width), LOW)
    down_full = run(lambda w, b: put(w, b, links.behind(0), 1), down_full, down_block)
    for k in range(3, ring):
        up_block = wait(up_next)
        if k < ring - 1:
            up_next = step(up_block)
            up_full = run(lambda w, b: put(w, b, links.behind(k), 0), up_full, up_block)
    down_next = step(down_block)
    if ring > 3:
        up_full = run(lambda w, b: put(w, b, links.behind(ring - 1), 0), up_full, up_block)

    def second_norm(tokens, low, cross):
        hidden = wide(tokens) + (wide(low) + wide(cross))
        standard, inverse = norm_forward(hidden)
        return hidden, standard, inverse, standard.astype(LOW)

    token_chunks = chunks(tokens)
    seconds, far_two, core_two, last_two = [], [], [], []
    normed_two = jnp.zeros((4 * rows, width), LOW)
    for j in range(2):
        out_cross[j] = wait(out_cross[j])
        seconds.append(run(second_norm, token_chunks[j], out_low[j], out_cross[j]))
        far_two.append(swap(seconds[j][3], 2))
        core_two.append(swap(seconds[j][3], 1))
        normed_two = run(lambda w, a: put_tokens(w, 0, a, j), normed_two, seconds[j][3])
    d_out_core, d_out_far[0] = wait(d_out_core, d_out_far[0])
    down_block = wait(down_next)
    if ring > 2:
        down_next = step(down_block)
    d_out_far.append(swap(d_out_chunks[1], 2))
    d_out_last = [swap(d_out_far[0], 1)]
    down_full, grad_plane = run(
        lambda w, b, g, x, y: (
            put(w, b, links.behind(1), 1),
            put_tokens(put_tokens(g, 1, x), 2, y, 0),
        ),
        down_full,
        down_block,
        grad_plane,
        d_out_core,
        d_out_far[0],
    )
    far_two[0], core_two[0] = wait(far_two[0], core_two[0])
    last_two.append(swap(far_two[0], 1))
    normed_two = run(
        lambda w, a, b: put_tokens(put_tokens(w, 1, a, 0), 2, b, 0),
        normed_two,
        core_two[0],
        far_two[0],
    )
    for k in range(2, ring - 1):
        down_block = wait(down_next)
        down_next = step(down_block)
        down_full = run(lambda w, b: put(w, b, links.behind(k), 1), down_full, down_block)
    far_two[1], core_two[1], last_two[0] = wait(far_two[1], core_two[1], last_two[0])
    last_pieces = links.to_core(far_two[1])
    normed_two = run(
        lambda w, a, b, c: put_tokens(
            put_tokens(put_tokens(w, 1, a, 1), 2, b, 1), 3, c, 0
        ),
        normed_two,
        core_two[1],
        far_two[1],
        last_two[0],
    )
    last_pieces = wait(*last_pieces)
    normed_two = run(
        lambda w, *p: put_tokens(w, 3, jnp.concatenate(p), 1), normed_two, *last_pieces
    )
    d_out_far[1], d_out_last[0] = wait(d_out_far[1], d_out_last[0])
    d_out_pieces = links.to_core(d_out_far[1])

    def feed_up(normed, weights):
        activated, slope = gelu_parts(plain(normed, weights))
        return activated.astype(LOW), slope.astype(LOW)

    act_low, slope = run(feed_up, normed_two, up_full)

    def part_down(act, grad, k, *arrived):
        part = inner(act, take(grad, links.behind(k), block, 1))
        for total in arrived:
            part = part + wide(total)
        return part.astype(LOW) if k < ring else part

    def part_up(normed, grad, k, *arrived):
        part = inner(take(normed, links.behind(k), block, 1), grad)
        for total in arrived:
            part = part + wide(total)
        return part.astype(LOW) if k < ring else part

    def ring_down(k, *arrived):
        total = run(lambda a, g, *t: part_down(a, g, k, *t), act_low, grad_plane, *arrived)
        return step(total) if k < ring else total

    def ring_up(k, *arrived):
        total = run(lambda n, g, *t: part_up(n, g, k, *t), normed_two, grad_pre, *arrived)
        return step(total) if k < ring else total

    d_out_pieces = wait(*d_out_pieces)
    grad_plane = run(
        lambda w, a, b, *p: put_tokens(
            put_tokens(put_tokens(w, 2, a, 1), 3, b, 0), 3, jnp.concatenate(p), 1
        ),
        grad_plane,
        d_out_far[1],
        d_out_last[0],
        *d_out_pieces,
    )
    down_sum = ring_down(1)
    if ring > 2:
        down_block = wait(down_next)
        down_full = run(lambda w, b: put(w, b, links.behind(ring - 1), 1), down_full, down_block)
    grad_pre = run(
        lambda g, w, s: (outer(g, w) * wide(s)).astype(LOW), grad_plane, down_full, slope
    )

    def near_sum(near, far):
        return (near + wide(far)).astype(LOW)

    last_n = [links.to_core(v) for v in run(low_part_of(outer, 3), grad_pre, up_full)]
    far_n = run(part_of(outer, 2), grad_pre, up_full)
    far_a = run(add_pieces_low, far_n[0], *wait(*last_n[0]))
    far_b = run(add_pieces_low, far_n[1], *wait(*last_n[1]))
    far_a = swap(far_a, 2)
    up_sum = ring_up(1)
    down_arrived = wait(down_sum)
    down_sum = ring_down(2, down_arrived)
    far_n = [far_a, swap(far_b, 2)]
    core_n = [links.to_core(v) for v in run(low_part_of(outer, 1), grad_pre, up_full)]
    own_n = run(part_of(outer, 0), grad_pre, up_full)
    near_n = [run(add_pieces, own_n[j], *wait(*core_n[j])) for j in range(2)]
    def second_back(d_out, low, cross, standard, inverse):
        scaled = wide(low) + wide(cross)
        grad_hidden = wide(d_out) + norm_backward(scaled, standard, inverse)
        return grad_hidden, grad_hidden.astype(LOW)

    def back_chunk(j):
        grad, low = run(
            second_back, d_out_chunks[j], low_n[j], cross_n[j], seconds[j][1], seconds[j][2]
        )
        return grad, low, links.to_core(low)

    low_n, cross_n = [], []
    for j in range(2):
        low_n.append(run(near_sum, near_n[j], wait(far_n[j])))
        cross_n.append(across(low_n[j]))
    cross_n[0] = wait(cross_n[0])
    backs = [back_chunk(0)]
    up_arrived = wait(up_sum)
    up_sum = ring_up(2, up_arrived)
    last_r = [links.to_core(v) for v in run(low_part_of(plain, 3), act_low, down_full)]
    core_r = [links.to_core(v) for v in run(low_part_of(plain, 1), act_low, down_full)]
    far_r = run(part_of(plain, 2), act_low, down_full)
    own_r = run(part_of(plain, 0), act_low, down_full)
    far_r = [swap(run(add_pieces_low, far_r[j], *wait(*last_r[j])), 2) for j in range(2)]
    near_r = [run(add_pieces, own_r[j], *wait(*core_r[j])) for j in range(2)]
    cross_n[1] = wait(cross_n[1])
    backs.append(back_chunk(1))
    grad_hidden = [backs[0][0], backs[1][0]]
    down_arrived = wait(down_sum)
    down_sum = ring_down(3, down_arrived)
    pieces = wait(*backs[0][2], *backs[1][2])
    grad_low = run(lambda *p: jnp.concatenate(p, axis=0), backs[0][1], backs[1][1], *pieces)

    def part_qkv(normed, grad, k):
        part = inner(take(normed, links.behind(k), block, 1), grad)
        return take(part, links.row, pair, 0), take(part, 1 - links.row, pair, 0).astype(LOW)

    def part_out(attended, grad, k):
        part = inner(attended, take(grad, links.behind(k), block, 1))
        return take(part, links.row, pair, 1), take(part, 1 - links.row, pair, 1).astype(LOW)

    out_owns, out_fars = [], []
    for k in range(1, ring + 1):
        own, far = run(lambda a, g: part_out(a, g, k), attended, grad_low)
        out_owns.append(own)
        out_fars.append(swap(far, 2))

    up_arrived = wait(up_sum)
    up_sum = ring_up(3, up_arrived)
    grad_att = run(lambda g, w: outer(g, w).astype(LOW), grad_low, out_full)
    grad_qkv = run(
        lambda q, d, f, g: jnp.concatenate(attention_call(attention_backward, q, d, f, g), axis=1),
        qkv,
        docs,
        frames,
        grad_att,
    )

    def add_row(own, far, *arrived):
        total = own + wide(far)
        for part in arrived:
            total = total + wide(part)
        return total

    def add_low(*parts):
        return add_row(*parts).astype(LOW)

    def cut(total, axis, size):
        parts = [take(total, links.cell, size, axis)]
        parts += [take(total, links.cell ^ k, size, axis).astype(LOW) for k in (1, 2, 3)]
        return tuple(parts)

    def up_end(gain, weight, *parts):
        raw = links.join([wide(part) for part in parts], 1)
        return raw * gain[:, None], jnp.sum(wide(weight) * raw, axis=1)

    def first_back(tokens, grads, lows, crosses):
        standard, inverse = norm_forward(wide(tokens))
        scaled = wide(jnp.concatenate(lows)) + wide(jnp.concatenate(crosses))
        return jnp.concatenate(grads) + norm_backward(scaled, standard, inverse)

    down_arrived = wait(down_sum)
    qkv_owns, qkv_fars = [], []
    for k in range(1, ring + 1):
        own, far = run(lambda n, g: part_qkv(n, g, k), normed_one, grad_qkv)
        qkv_owns.append(own)
        qkv_fars.append(swap(far, 2) if k == 1 else far)
    *out_fars, far_r[0], far_r[1] = wait(*out_fars, *far_r)
    low_r = [run(near_sum, near_r[j], far_r[j]) for j in range(2)]
    cross_r = [across(part) for part in low_r]
    for k in range(4, ring + 1):
        down_sum = ring_down(k, down_arrived)
        if k < ring:
            down_arrived = wait(down_sum)
    down_ends = list(run(lambda t: cut(t, 1, owned), down_sum))
    down_ends[1], down_ends[2] = swap(down_ends[1], 1), swap(down_ends[2], 2)
    up_arrived = wait(up_sum)
    for k in range(4, ring + 1):
        up_sum = ring_up(k, up_arrived)
        if k < ring:
            up_arrived = wait(up_sum)
    up_ends = list(run(lambda t: cut(t, 0, owned), up_sum))

    qkv_fars[0], down_ends[1], down_ends[2] = wait(qkv_fars[0], down_ends[1], down_ends[2])
    qkv_sum, out_sum = run(
        lambda a, b, c, d: (add_low(a, b), add_low(c, d)),
        qkv_owns[0],
        qkv_fars[0],
        out_owns[0],
        out_fars[0],
    )
    for k in range(2, ring + 1):
        sent = [step(qkv_sum), step(out_sum), swap(qkv_fars[k - 1], 2)]
        if k == 2:
            down_ends[3] = swap(down_ends[3], 3)
            core_m = [links.to_core(v) for v in run(low_part_of(outer, 1), grad_qkv, qkv_full)]
            own_m = run(part_of(outer, 0), grad_qkv, qkv_full)
            low_m = [run(add_pieces_low, own_m[j], *wait(*core_m[j])) for j in range(2)]
            cross_m = [across(part) for part in low_m]
            *sent, down_ends[3], cross_r[0], cross_r[1] = wait(*sent, down_ends[3], *cross_r)
        elif k == 3:
            up_ends[1], up_ends[2] = swap(up_ends[1], 1), swap(up_ends[2], 2)
            result = run(
                lambda *p: jnp.concatenate(p[:2])
                + (wide(jnp.concatenate(p[2:4])) + wide(jnp.concatenate(p[4:]))),
                seconds[0][0],
                seconds[1][0],
                *low_r,
                *cross_r,
            )
            d_w_down = run(lambda *p: links.join([wide(part) for part in p], 0), *down_ends)
            *sent, up_ends[1], up_ends[2], cross_m[0], cross_m[1] = wait(
                *sent, up_ends[1], up_ends[2], *cross_m
            )
        elif k == 4:
            up_ends[3] = swap(up_ends[3], 3)
            d_tokens = run(
                lambda t, *p: first_back(t, p[:2], p[2:4], p[4:]),
                tokens,
                *grad_hidden,
                *low_m,
                *cross_m,
            )
            *sent, up_ends[3] = wait(*sent, up_ends[3])
        else:
            sent = wait(*sent)
        add = add_low if k < ring else add_row
        qkv_sum, out_sum = run(
            lambda *p: (add(*p[:3]), add(*p[3:])),
            qkv_owns[k - 1],
            sent[2],
            sent[0],
            out_owns[k - 1],
            out_fars[k - 1],
            sent[1],
        )

    def ends(qkv, out):
        return (
            take(qkv, links.core, owned, 0),
            take(qkv, 1 - links.core, owned, 0).astype(LOW),
            take(out, links.core, owned, 1),
            take(out, 1 - links.core, owned, 1).astype(LOW),
        )

    qkv_mine, qkv_yours, out_mine, out_yours = run(ends, qkv_sum, out_sum)
    qkv_yours, out_yours = swap(qkv_yours, 1), swap(out_yours, 1)
    d_w_up, gain_mlp_own = run(up_end, gain_mlp, w_up, *up_ends)
    gain_mlp_other = across(gain_mlp_own)
    qkv_yours, out_yours = wait(qkv_yours, out_yours)
    d_w_output = links.by_core(out_mine, wide(out_yours), 0)
    raw = [
        links.by_core(qkv_mine[:, at : at + half], wide(qkv_yours[:, at : at + half]), 1)
        for at in (0, half, 2 * half)
    ]
    gain_attn_own = sum(
        jnp.sum(wide(weight) * part, axis=1) for weight, part in zip((w_query, w_key, w_value), raw)
    )
    gain_attn_other = across(gain_attn_own)
    d_gain_attn = gain_attn_own + gain_attn_other
    d_gain_mlp = gain_mlp_own + gain_mlp_other
    d_w_query, d_w_key, d_w_value = (part * gain_attn[:, None] for part in raw)
    return (
        result,
        d_tokens,
        d_gain_attn,
        d_w_query,
        d_w_key,
        d_w_value,
        d_w_output,
        d_gain_mlp,
        d_w_up,
        d_w_down,
    )


def solution(mesh):
    return jax.shard_map(
        functools.partial(shards, mesh.shape["dp"]),
        mesh=mesh,
        in_specs=(
            P("dp", None),
            P("dp", None),
            P("dp", None),
            P("dp"),
            P("dp", "mp"),
            P("dp", "mp"),
            P("dp", "mp"),
            P("mp", "dp"),
            P("dp"),
            P("dp", "mp"),
            P("mp", "dp"),
            P("dp", None),
        ),
        out_specs=(
            P("dp", None),
            P("dp", None),
            P("dp"),
            P("dp", "mp"),
            P("dp", "mp"),
            P("dp", "mp"),
            P("mp", "dp"),
            P("dp"),
            P("dp", "mp"),
            P("mp", "dp"),
        ),
        check_vma=False,
    )
```

```python
import functools
import math

import jax
import jax.numpy as jnp
from jax import lax
from jax.experimental import pallas as pl
from jax.experimental.pallas import tpu as pltpu
from jax.sharding import PartitionSpec as P

HEAD_DIM = 128
EPSILON = 1e-05
MASKED = -1e30
PIECE = 96
LOW = jnp.bfloat16
WIDE = jnp.float32


def plain(one, two):
    return jnp.dot(one, two, preferred_element_type=WIDE)


def inner(one, two):
    return lax.dot_general(one, two, (((0,), (0,)), ((), ())), preferred_element_type=WIDE)


def outer(one, two):
    return lax.dot_general(one, two, (((1,), (1,)), ((), ())), preferred_element_type=WIDE)


def norm_forward(values):
    centered = values - jnp.mean(values, axis=1, keepdims=True)
    inverse = lax.rsqrt(jnp.mean(centered * centered, axis=1, keepdims=True) + EPSILON)
    return centered * inverse, inverse


def norm_backward(scaled, standard, inverse):
    return (
        scaled
        - jnp.mean(scaled, axis=1, keepdims=True)
        - standard * jnp.mean(scaled * standard, axis=1, keepdims=True)
    ) * inverse


def gelu_parts(values):
    half = 0.5 * (1.0 + lax.erf(values * (1.0 / math.sqrt(2.0))))
    slope = half + values * jnp.exp(-0.5 * values * values) * (1.0 / math.sqrt(2.0 * math.pi))
    return values * half, slope


def take(values, index, size, axis):
    return lax.dynamic_slice_in_dim(values, index * size, size, axis)


def put(whole, part, index, axis):
    return lax.dynamic_update_slice_in_dim(whole, part, index * part.shape[axis], axis)


def wide(values):
    return values.astype(WIDE)


def unscaled_probs(query, key, allowed):
    scores = jnp.where(allowed, outer(query, key) * (1.0 / math.sqrt(HEAD_DIM)), MASKED)
    shifted = jnp.exp(scores - jnp.max(scores, axis=1, keepdims=True))
    return shifted, 1.0 / jnp.sum(shifted, axis=1, keepdims=True)


def head_cuts(heads):
    return [slice(i * HEAD_DIM, (i + 1) * HEAD_DIM) for i in range(heads)]


def attention_forward(query, key, value, doc_row, doc_col, frame_row, frame_col, out):
    allowed = (doc_col[0] == doc_row[0]) & (frame_row[0] <= frame_col[0])
    for cut in head_cuts(out.shape[1] // HEAD_DIM):
        shifted, inverse = unscaled_probs(query[:, cut], key[:, cut], allowed)
        out[:, cut] = plain((shifted * inverse).astype(LOW), value[:, cut]).astype(LOW)


def attention_backward(
    query, key, value, grad, doc_row, doc_col, frame_row, frame_col, to_query, to_key, to_value
):
    allowed = (doc_col[0] == doc_row[0]) & (frame_row[0] <= frame_col[0])
    factor = 1.0 / math.sqrt(HEAD_DIM)
    for cut in head_cuts(grad.shape[1] // HEAD_DIM):
        shifted, inverse = unscaled_probs(query[:, cut], key[:, cut], allowed)
        probs = shifted * inverse
        grad_probs = outer(grad[:, cut], value[:, cut])
        delta = jnp.sum(grad_probs * probs, axis=1, keepdims=True)
        grad_scores = (probs * (grad_probs - delta)).astype(LOW)
        to_query[:, cut] = (plain(grad_scores, key[:, cut]) * factor).astype(LOW)
        to_key[:, cut] = (inner(grad_scores, query[:, cut]) * factor).astype(LOW)
        to_value[:, cut] = inner(probs.astype(LOW), grad[:, cut]).astype(LOW)


def attention_call(kernel, qkv, docs, frames, *grads):
    rows, half = qkv.shape[0] // 2, qkv.shape[1] // 3
    parts = [pl.BlockSpec((rows, half), lambda g, at=at: (g, at)) for at in range(3)]
    along = pl.BlockSpec((1, 1, rows), lambda g: (g, 0, 0))
    down = pl.BlockSpec((1, rows, 1), lambda g: (g, 0, 0))
    shape = jax.ShapeDtypeStruct((2 * rows, half), LOW)
    outs = 3 if grads else 1
    return pl.pallas_call(
        kernel,
        out_shape=[shape] * outs,
        grid=(2,),
        in_specs=parts + parts[:1] * len(grads) + [along, down, along, down],
        out_specs=parts[:1] * outs,
        compiler_params=pltpu.CompilerParams(vmem_limit_bytes=32 << 20),
        cost_estimate=pl.CostEstimate(flops=0, bytes_accessed=0, transcendentals=0),
    )(
        qkv,
        qkv,
        qkv,
        *grads,
        docs[:, None, :],
        docs[:, :, None],
        frames[:, None, :],
        frames[:, :, None],
    )


class Order:
    def __init__(self, token):
        self.token = token

    def tie(self, *values):
        tied = lax.optimization_barrier((*values, self.token))[:-1]
        return tied if len(tied) > 1 else tied[0]

    def wait(self, *values):
        *values, self.token = lax.optimization_barrier((*values, self.token))
        return values if len(values) > 1 else values[0]

    def run(self, step, *values):
        values = lax.optimization_barrier((*values, self.token))[:-1]
        results = step(*values)
        if not isinstance(results, tuple):
            return self.wait(results)
        return self.wait(*results)


class Links:
    def __init__(self, count, order):
        self.order = order
        self.ring_size = count // 4
        self.to = {k: [(i, i ^ k) for i in range(count)] for k in (1, 2, 3)}
        self.next = [(i, (i + 4) % count) for i in range(count)]
        place = lax.axis_index("dp")
        self.ring_at = place // 4
        self.cell = place % 4
        self.row = self.cell // 2
        self.core = self.cell % 2

    def swap(self, values, k):
        return lax.ppermute(self.order.tie(values), "dp", self.to[k])

    def to_core(self, values):
        size = values.shape[0] // max(1, values.shape[0] // PIECE)
        return [self.swap(values[at : at + size], 1) for at in range(0, values.shape[0], size)]

    def step(self, values):
        return lax.ppermute(self.order.tie(values), "dp", self.next)

    def across(self, values):
        return lax.ppermute(self.order.tie(values), "mp", [(0, 1), (1, 0)])

    def behind(self, k):
        return lax.rem(self.ring_at - k + 2 * self.ring_size, self.ring_size)

    def by_core(self, own, other, axis):
        return jnp.where(
            self.core == 0,
            jnp.concatenate([own, other], axis=axis),
            jnp.concatenate([other, own], axis=axis),
        )

    def join(self, parts, axis):
        shape = list(parts[0].shape)
        shape[axis] *= len(parts)
        joined = jnp.zeros(shape, parts[0].dtype)
        for k, part in enumerate(parts):
            joined = put(joined, part, self.cell ^ k, axis)
        return joined

    def lay(self, blocks, axis):
        shape = list(blocks[0].shape)
        shape[axis] *= len(blocks)
        whole = jnp.zeros(shape, blocks[0].dtype)
        for k, block in enumerate(blocks):
            whole = put(whole, block, self.behind(k), axis)
        return whole

    def lay_pairs(self, near, far, axis):
        shape = list(near[0].shape)
        shape[axis] *= 2 * len(near)
        whole = jnp.zeros(shape, near[0].dtype)
        for k in range(len(near)):
            at = self.behind(k) * 2
            whole = put(whole, near[k], at + self.row, axis)
            whole = put(whole, far[k], at + 1 - self.row, axis)
        return whole


def shards(
    count,
    tokens,
    doc_ids,
    frame_ids,
    gain_attn,
    w_query,
    w_key,
    w_value,
    w_output,
    gain_mlp,
    w_up,
    w_down,
    d_out,
):
    order = Order(doc_ids)
    run, wait = order.run, order.wait
    links = Links(count, order)
    swap, step, across = links.swap, links.step, links.across
    ring = links.ring_size
    rows, width = tokens.shape
    owned = width // count
    half = w_query.shape[1] // 2
    heads = half // HEAD_DIM
    hidden_part = w_up.shape[1] // 4
    block = width // ring
    pair = block // 2
    others = range(1, ring)

    chunk = rows // 2

    def chunks(values):
        return values[:chunk], values[chunk:]

    def qkv_shard(core, gain, *weights):
        taken = [(wide(take(w, core, half, 1)) * gain[:, None]).astype(LOW) for w in weights]
        return jnp.concatenate(taken, axis=1)

    qkv_send = run(
        lambda *w: qkv_shard(1 - links.core, *w), gain_attn, w_query, w_key, w_value
    )
    qkv_other = swap(qkv_send, 1)
    out_other = swap(run(lambda w: take(w, 1 - links.core, half, 0), w_output), 1)
    qkv_own = run(lambda *w: qkv_shard(links.core, *w), gain_attn, w_query, w_key, w_value)
    qkv_other, out_other = wait(qkv_other, out_other)
    qkv_block, out_block = run(
        lambda a, b, w, o: (
            links.by_core(a, b, 0),
            links.by_core(take(w, links.core, half, 0), o, 1),
        ),
        qkv_own,
        qkv_other,
        w_output,
        out_other,
    )

    def up_shard(weight, gain):
        scaled = (wide(weight) * gain[:, None]).astype(LOW)
        return tuple(take(scaled, links.cell ^ k, hidden_part, 1) for k in (0, 2, 1, 3))

    def put_near(whole, part, k, axis):
        return put(whole, part, links.behind(k) * 2 + links.row, axis)

    def put_far(whole, part, k, axis):
        return put(whole, part, links.behind(k) * 2 + 1 - links.row, axis)

    qkv_next, out_next, qkv_far = step(qkv_block), step(out_block), swap(qkv_block, 2)
    up_own, up_row, up_core, up_last = run(up_shard, w_up, gain_mlp)
    up_row, up_core = swap(up_row, 2), swap(up_core, 1)
    normed_own = run(lambda x: norm_forward(wide(x))[0].astype(LOW), tokens)
    normed_other = swap(normed_own, 1)
    docs_other, frames_other = swap(doc_ids, 1), swap(frame_ids, 1)
    qkv_full = jnp.zeros((width, 3 * half), LOW)
    out_full = jnp.zeros((half, width), LOW)
    qkv_full, out_full = run(
        lambda q, o, a, b: (put_near(q, a, 0, 0), put_near(o, b, 0, 1)),
        qkv_full,
        out_full,
        qkv_block,
        out_block,
    )
    down_own, down_row, down_core, down_last = run(
        lambda w: tuple(take(w, links.cell ^ k, hidden_part, 0) for k in (0, 2, 1, 3)), w_down
    )
    out_blocks = [out_block]
    for k in others:
        arriving = [qkv_next, out_next, qkv_far]
        if k == 1:
            arriving += [up_row, up_core]
        if k == 2:
            arriving += [up_last]
        if k == 3:
            arriving += [out_far]
        qkv_block, out_block, far_arrived, *arrived = wait(*arriving)
        if k < ring - 1:
            qkv_next, out_next = step(qkv_block), step(out_block)
        elif ring > 2:
            up_next = step(up_block)
        qkv_far = swap(qkv_block, 2)
        out_blocks.append(out_block)
        if k == 1:
            up_row, up_core = arrived
            up_last = swap(up_last, 3)
        if k == 2:
            (up_last,) = arrived
            out_far = swap(out_blocks[0], 2)
        if k == 3:
            (out_far,) = arrived
        if k == ring - 1:
            down_row, down_core = swap(down_row, 2), swap(down_core, 1)
        qkv_full, out_full = run(
            lambda q, o, a, b, f: (
                put_far(put_near(q, a, k, 0), f, k - 1, 0),
                put_near(o, b, k, 1),
            ),
            qkv_full,
            out_full,
            qkv_block,
            out_block,
            far_arrived,
        )
        if k == min(2, ring - 1):
            if ring < 3:
                up_last = wait(up_last)
            up_block = run(lambda *p: links.join(p, 0), up_own, up_core, up_row, up_last)
            if ring < 3:
                up_next = step(up_block)
        if k == 3:
            out_full = run(lambda o, f: put_far(o, f, 0, 1), out_full, out_far)
    normed_other, docs_other, frames_other = wait(normed_other, docs_other, frames_other)
    normed_one = run(lambda a, b: jnp.concatenate([a, b], axis=0), normed_own, normed_other)
    up_full = jnp.zeros((width, hidden_part), LOW)
    up_full = run(lambda w, b: put(w, b, links.behind(0), 0), up_full, up_block)
    up_block, qkv_far, down_row, down_core = wait(up_next, qkv_far, down_row, down_core)
    if ring > 2:
        up_next = step(up_block)
    fars_from = 1 if ring > 3 else 0
    out_fars = [swap(out_blocks[k], 2) for k in range(fars_from, ring)]
    down_last = swap(down_last, 3)
    d_out_core = swap(d_out, 1)
    qkv_full = run(lambda w, f: put_far(w, f, ring - 1, 0), qkv_full, qkv_far)
    qkv = run(lambda a, b: plain(a, b).astype(LOW), normed_one, qkv_full)

    docs = jnp.concatenate([doc_ids, docs_other], axis=0)
    frames = jnp.concatenate([frame_ids, frames_other], axis=0)
    docs, frames = wait(docs, frames)
    attended = run(lambda *v: attention_call(attention_forward, *v)[0], qkv, docs, frames)
    if ring > 2:
        up_arrived, down_last, *out_fars = wait(up_next, down_last, *out_fars)
        if ring > 3:
            up_next = step(up_arrived)
    else:
        up_arrived = up_block
        down_last, *out_fars = wait(down_last, *out_fars)
    d_out_chunks = chunks(d_out)
    d_out_far = [swap(d_out_chunks[0], 2)]

    def put_fars(whole, *fars):
        for k, far in enumerate(fars):
            whole = put_far(whole, far, fars_from + k, 1)
        return whole

    out_full = run(put_fars, out_full, *out_fars)

    def part_of(product, group):
        return lambda left, weights: chunks(
            product(left[group * rows : (group + 1) * rows], weights)
        )

    def low_part_of(product, group):
        part = part_of(product, group)
        return lambda left, weights: tuple(value.astype(LOW) for value in part(left, weights))

    def add_pieces(own, *pieces):
        return own + wide(jnp.concatenate(pieces))

    def add_pieces_low(own, *pieces):
        return add_pieces(own, *pieces).astype(LOW)

    yours = [links.to_core(v) for v in run(low_part_of(plain, 1), attended, out_full)]
    mine = run(part_of(plain, 0), attended, out_full)
    out_low, out_cross = [], []
    for j in range(2):
        out_low.append(run(add_pieces_low, mine[j], *wait(*yours[j])))
        out_cross.append(across(out_low[j]))
    down_block = run(lambda *p: links.join(p, 1), down_own, down_core, down_row, down_last)
    up_full = run(
        lambda w, a, b: put(put(w, a, links.behind(1), 0), b, links.behind(min(2, ring - 1)), 0),
        up_full,
        up_block,
        up_arrived,
    )

    def put_tokens(whole, group, part, *chunk_at):
        at = group * rows + (chunk * chunk_at[0] if chunk_at else 0)
        return lax.dynamic_update_slice_in_dim(whole, part, at, 0)

    grad_plane = jnp.zeros((4 * rows, width), LOW)
    grad_plane = run(lambda w, a: put_tokens(w, 0, a), grad_plane, d_out)
    down_full = jnp.zeros((hidden_part, width), LOW)
    down_full = run(lambda w, b: put(w, b, links.behind(0), 1), down_full, down_block)
    for k in range(3, ring):
        up_block = wait(up_next)
        if k < ring - 1:
            up_next = step(up_block)
            up_full = run(lambda w, b: put(w, b, links.behind(k), 0), up_full, up_block)
    down_next = step(down_block)
    if ring > 3:
        up_full = run(lambda w, b: put(w, b, links.behind(ring - 1), 0), up_full, up_block)

    def second_norm(tokens, low, cross):
        hidden = wide(tokens) + (wide(low) + wide(cross))
        standard, inverse = norm_forward(hidden)
        return hidden, standard, inverse, standard.astype(LOW)

    token_chunks = chunks(tokens)
    seconds, far_two, core_two, last_two = [], [], [], []
    normed_two = jnp.zeros((4 * rows, width), LOW)
    for j in range(2):
        out_cross[j] = wait(out_cross[j])
        seconds.append(run(second_norm, token_chunks[j], out_low[j], out_cross[j]))
        far_two.append(swap(seconds[j][3], 2))
        core_two.append(swap(seconds[j][3], 1))
        normed_two = run(lambda w, a: put_tokens(w, 0, a, j), normed_two, seconds[j][3])
    d_out_core, d_out_far[0] = wait(d_out_core, d_out_far[0])
    down_block = wait(down_next)
    if ring > 2:
        down_next = step(down_block)
    d_out_far.append(swap(d_out_chunks[1], 2))
    d_out_last = [swap(d_out_far[0], 1)]
    down_full, grad_plane = run(
        lambda w, b, g, x, y: (
            put(w, b, links.behind(1), 1),
            put_tokens(put_tokens(g, 1, x), 2, y, 0),
        ),
        down_full,
        down_block,
        grad_plane,
        d_out_core,
        d_out_far[0],
    )
    far_two[0], core_two[0] = wait(far_two[0], core_two[0])
    last_two.append(swap(far_two[0], 1))
    normed_two = run(
        lambda w, a, b: put_tokens(put_tokens(w, 1, a, 0), 2, b, 0),
        normed_two,
        core_two[0],
        far_two[0],
    )
    for k in range(2, ring - 1):
        down_block = wait(down_next)
        down_next = step(down_block)
        down_full = run(lambda w, b: put(w, b, links.behind(k), 1), down_full, down_block)
    far_two[1], core_two[1], last_two[0] = wait(far_two[1], core_two[1], last_two[0])
    last_pieces = links.to_core(far_two[1])
    normed_two = run(
        lambda w, a, b, c: put_tokens(
            put_tokens(put_tokens(w, 1, a, 1), 2, b, 1), 3, c, 0
        ),
        normed_two,
        core_two[1],
        far_two[1],
        last_two[0],
    )
    last_pieces = wait(*last_pieces)
    normed_two = run(
        lambda w, *p: put_tokens(w, 3, jnp.concatenate(p), 1), normed_two, *last_pieces
    )
    d_out_far[1], d_out_last[0] = wait(d_out_far[1], d_out_last[0])
    d_out_pieces = links.to_core(d_out_far[1])

    def feed_up(normed, weights):
        activated, slope = gelu_parts(plain(normed, weights))
        return activated.astype(LOW), slope.astype(LOW)

    act_low, slope = run(feed_up, normed_two, up_full)

    def part_down(act, grad, k, *arrived):
        part = inner(act, take(grad, links.behind(k), block, 1))
        for total in arrived:
            part = part + wide(total)
        return part.astype(LOW) if k < ring else part

    def part_up(normed, grad, k, *arrived):
        part = inner(take(normed, links.behind(k), block, 1), grad)
        for total in arrived:
            part = part + wide(total)
        return part.astype(LOW) if k < ring else part

    def ring_down(k, *arrived):
        total = run(lambda a, g, *t: part_down(a, g, k, *t), act_low, grad_plane, *arrived)
        return step(total) if k < ring else total

    def ring_up(k, *arrived):
        total = run(lambda n, g, *t: part_up(n, g, k, *t), normed_two, grad_pre, *arrived)
        return step(total) if k < ring else total

    d_out_pieces = wait(*d_out_pieces)
    grad_plane = run(
        lambda w, a, b, *p: put_tokens(
            put_tokens(put_tokens(w, 2, a, 1), 3, b, 0), 3, jnp.concatenate(p), 1
        ),
        grad_plane,
        d_out_far[1],
        d_out_last[0],
        *d_out_pieces,
    )
    down_sum = ring_down(1)
    if ring > 2:
        down_block = wait(down_next)
        down_full = run(lambda w, b: put(w, b, links.behind(ring - 1), 1), down_full, down_block)
    grad_pre = run(
        lambda g, w, s: (outer(g, w) * wide(s)).astype(LOW), grad_plane, down_full, slope
    )

    def near_sum(near, far):
        return (near + wide(far)).astype(LOW)

    last_n = [links.to_core(v) for v in run(low_part_of(outer, 3), grad_pre, up_full)]
    far_n = run(part_of(outer, 2), grad_pre, up_full)
    far_a = run(add_pieces_low, far_n[0], *wait(*last_n[0]))
    far_b = run(add_pieces_low, far_n[1], *wait(*last_n[1]))
    far_a = swap(far_a, 2)
    up_sum = ring_up(1)
    down_arrived = wait(down_sum)
    down_sum = ring_down(2, down_arrived)
    far_n = [far_a, swap(far_b, 2)]
    core_n = [links.to_core(v) for v in run(low_part_of(outer, 1), grad_pre, up_full)]
    own_n = run(part_of(outer, 0), grad_pre, up_full)
    near_n = [run(add_pieces, own_n[j], *wait(*core_n[j])) for j in range(2)]
    def second_back(d_out, low, cross, standard, inverse):
        scaled = wide(low) + wide(cross)
        grad_hidden = wide(d_out) + norm_backward(scaled, standard, inverse)
        return grad_hidden, grad_hidden.astype(LOW)

    def back_chunk(j):
        grad, low = run(
            second_back, d_out_chunks[j], low_n[j], cross_n[j], seconds[j][1], seconds[j][2]
        )
        return grad, low, links.to_core(low)

    low_n, cross_n = [], []
    for j in range(2):
        low_n.append(run(near_sum, near_n[j], wait(far_n[j])))
        cross_n.append(across(low_n[j]))
    cross_n[0] = wait(cross_n[0])
    backs = [back_chunk(0)]
    up_arrived = wait(up_sum)
    up_sum = ring_up(2, up_arrived)
    last_r = [links.to_core(v) for v in run(low_part_of(plain, 3), act_low, down_full)]
    core_r = [links.to_core(v) for v in run(low_part_of(plain, 1), act_low, down_full)]
    far_r = run(part_of(plain, 2), act_low, down_full)
    own_r = run(part_of(plain, 0), act_low, down_full)
    far_r = [swap(run(add_pieces_low, far_r[j], *wait(*last_r[j])), 2) for j in range(2)]
    near_r = [run(add_pieces, own_r[j], *wait(*core_r[j])) for j in range(2)]
    cross_n[1] = wait(cross_n[1])
    backs.append(back_chunk(1))
    grad_hidden = [backs[0][0], backs[1][0]]
    down_arrived = wait(down_sum)
    down_sum = ring_down(3, down_arrived)
    pieces = wait(*backs[0][2], *backs[1][2])
    grad_low = run(lambda *p: jnp.concatenate(p, axis=0), backs[0][1], backs[1][1], *pieces)

    def part_qkv(normed, grad, k):
        part = inner(take(normed, links.behind(k), block, 1), grad)
        return take(part, links.row, pair, 0), take(part, 1 - links.row, pair, 0).astype(LOW)

    def part_out(attended, grad, k):
        part = inner(attended, take(grad, links.behind(k), block, 1))
        return take(part, links.row, pair, 1), take(part, 1 - links.row, pair, 1).astype(LOW)

    out_owns, out_fars = [], []
    for k in range(1, ring + 1):
        own, far = run(lambda a, g: part_out(a, g, k), attended, grad_low)
        out_owns.append(own)
        out_fars.append(swap(far, 2))

    up_arrived = wait(up_sum)
    up_sum = ring_up(3, up_arrived)
    grad_att = run(lambda g, w: outer(g, w).astype(LOW), grad_low, out_full)
    grad_qkv = run(
        lambda q, d, f, g: jnp.concatenate(attention_call(attention_backward, q, d, f, g), axis=1),
        qkv,
        docs,
        frames,
        grad_att,
    )

    def add_row(own, far, *arrived):
        total = own + wide(far)
        for part in arrived:
            total = total + wide(part)
        return total

    def add_low(*parts):
        return add_row(*parts).astype(LOW)

    def cut(total, axis, size):
        parts = [take(total, links.cell, size, axis)]
        parts += [take(total, links.cell ^ k, size, axis).astype(LOW) for k in (1, 2, 3)]
        return tuple(parts)

    def up_end(gain, weight, *parts):
        raw = links.join([wide(part) for part in parts], 1)
        return raw * gain[:, None], jnp.sum(wide(weight) * raw, axis=1)

    def first_back(tokens, grads, lows, crosses):
        standard, inverse = norm_forward(wide(tokens))
        scaled = wide(jnp.concatenate(lows)) + wide(jnp.concatenate(crosses))
        return jnp.concatenate(grads) + norm_backward(scaled, standard, inverse)

    down_arrived = wait(down_sum)
    qkv_owns, qkv_fars = [], []
    for k in range(1, ring + 1):
        own, far = run(lambda n, g: part_qkv(n, g, k), normed_one, grad_qkv)
        qkv_owns.append(own)
        qkv_fars.append(swap(far, 2) if k == 1 else far)
    core_m = [links.to_core(v) for v in run(low_part_of(outer, 1), grad_qkv, qkv_full)]
    own_m = run(part_of(outer, 0), grad_qkv, qkv_full)
    low_m = [run(add_pieces_low, own_m[j], *wait(*core_m[j])) for j in range(2)]
    *out_fars, far_r[0], far_r[1] = wait(*out_fars, *far_r)
    low_r = [run(near_sum, near_r[j], far_r[j]) for j in range(2)]
    cross_r = [across(part) for part in low_r]
    for k in range(4, ring + 1):
        down_sum = ring_down(k, down_arrived)
        if k < ring:
            down_arrived = wait(down_sum)
    down_ends = list(run(lambda t: cut(t, 1, owned), down_sum))
    down_ends[1], down_ends[2] = swap(down_ends[1], 1), swap(down_ends[2], 2)
    up_arrived = wait(up_sum)
    for k in range(4, ring + 1):
        up_sum = ring_up(k, up_arrived)
        if k < ring:
            up_arrived = wait(up_sum)
    up_ends = list(run(lambda t: cut(t, 0, owned), up_sum))

    qkv_fars[0], down_ends[1], down_ends[2] = wait(qkv_fars[0], down_ends[1], down_ends[2])
    qkv_sum, out_sum = run(
        lambda a, b, c, d: (add_low(a, b), add_low(c, d)),
        qkv_owns[0],
        qkv_fars[0],
        out_owns[0],
        out_fars[0],
    )
    for k in range(2, ring + 1):
        sent = [step(qkv_sum), step(out_sum), swap(qkv_fars[k - 1], 2)]
        if k == 2:
            down_ends[3] = swap(down_ends[3], 3)
            cross_m = [across(part) for part in low_m]
            *sent, down_ends[3], cross_r[0], cross_r[1] = wait(*sent, down_ends[3], *cross_r)
        elif k == 3:
            up_ends[1], up_ends[2] = swap(up_ends[1], 1), swap(up_ends[2], 2)
            result = run(
                lambda *p: jnp.concatenate(p[:2])
                + (wide(jnp.concatenate(p[2:4])) + wide(jnp.concatenate(p[4:]))),
                seconds[0][0],
                seconds[1][0],
                *low_r,
                *cross_r,
            )
            d_w_down = run(lambda *p: links.join([wide(part) for part in p], 0), *down_ends)
            *sent, up_ends[1], up_ends[2], cross_m[0], cross_m[1] = wait(
                *sent, up_ends[1], up_ends[2], *cross_m
            )
        elif k == 4:
            up_ends[3] = swap(up_ends[3], 3)
            d_tokens = run(
                lambda t, *p: first_back(t, p[:2], p[2:4], p[4:]),
                tokens,
                *grad_hidden,
                *low_m,
                *cross_m,
            )
            *sent, up_ends[3] = wait(*sent, up_ends[3])
        else:
            sent = wait(*sent)
        add = add_low if k < ring else add_row
        qkv_sum, out_sum = run(
            lambda *p: (add(*p[:3]), add(*p[3:])),
            qkv_owns[k - 1],
            sent[2],
            sent[0],
            out_owns[k - 1],
            out_fars[k - 1],
            sent[1],
        )

    def ends(qkv, out):
        return (
            take(qkv, links.core, owned, 0),
            take(qkv, 1 - links.core, owned, 0).astype(LOW),
            take(out, links.core, owned, 1),
            take(out, 1 - links.core, owned, 1).astype(LOW),
        )

    qkv_mine, qkv_yours, out_mine, out_yours = run(ends, qkv_sum, out_sum)
    qkv_yours, out_yours = swap(qkv_yours, 1), swap(out_yours, 1)
    d_w_up, gain_mlp_own = run(up_end, gain_mlp, w_up, *up_ends)
    gain_mlp_other = across(gain_mlp_own)
    qkv_yours, out_yours = wait(qkv_yours, out_yours)
    d_w_output = links.by_core(out_mine, wide(out_yours), 0)
    raw = [
        links.by_core(qkv_mine[:, at : at + half], wide(qkv_yours[:, at : at + half]), 1)
        for at in (0, half, 2 * half)
    ]
    gain_attn_own = sum(
        jnp.sum(wide(weight) * part, axis=1) for weight, part in zip((w_query, w_key, w_value), raw)
    )
    gain_attn_other = across(gain_attn_own)
    d_gain_attn = gain_attn_own + gain_attn_other
    d_gain_mlp = gain_mlp_own + gain_mlp_other
    d_w_query, d_w_key, d_w_value = (part * gain_attn[:, None] for part in raw)
    return (
        result,
        d_tokens,
        d_gain_attn,
        d_w_query,
        d_w_key,
        d_w_value,
        d_w_output,
        d_gain_mlp,
        d_w_up,
        d_w_down,
    )


def solution(mesh):
    return jax.shard_map(
        functools.partial(shards, mesh.shape["dp"]),
        mesh=mesh,
        in_specs=(
            P("dp", None),
            P("dp", None),
            P("dp", None),
            P("dp"),
            P("dp", "mp"),
            P("dp", "mp"),
            P("dp", "mp"),
            P("mp", "dp"),
            P("dp"),
            P("dp", "mp"),
            P("mp", "dp"),
            P("dp", None),
        ),
        out_specs=(
            P("dp", None),
            P("dp", None),
            P("dp"),
            P("dp", "mp"),
            P("dp", "mp"),
            P("dp", "mp"),
            P("mp", "dp"),
            P("dp"),
            P("dp", "mp"),
            P("mp", "dp"),
        ),
        check_vma=False,
    )
```
